32 devices in a mesh: freq: 4 (over y, x), mat: 8 (over z, core).
Axes of the slice: x: 2, y: 2, z: 4, core: 2. Of those that a mesh axis runs over, the one named last changes fastest.
Arguments:
- traces: bfloat16 [2048, 64, 4096], P('freq', None, 'mat'), may hold values from -6 to 6
- reflection: bfloat16 [8, 2, 4096, 4096], P('freq', None, 'mat'), may hold values from -0.0625 to 0.0625
- onset: int32 [64, 4096], P(None, 'mat'), may hold values from 512 to 2047
Outputs:
- windowed: bfloat16 [2048, 64, 4096], P('freq', None, 'mat')
The draws below stay inside these ranges and needn't reach their ends.
Inputs may be any that keep to these rules, and one draw needn't show every extreme that they name: onset sample of the direct arrival for each focal point and receiver.
All inputs are finite; a program needn't handle non-finite values.
Results may differ from the reference program's by a relative error of at most 0.0069.
Values may be sent and summed in bfloat16 or wider, within the bound.
No kernel may reach another device: no remote copies, remote signals or barrier semaphores. Data moves between devices by JAX's collectives and lax.ppermute only.
A program may use at most 192 MiB of HBM per device.

```python
import math
import jax
import jax.numpy as jnp
from jax import lax

NR = 4096
NT = 2048
P_SIZE = 64
NF = 8
N_FREQ = 4


def plant(array, key, smallest, top_value):
    spot = [jax.random.randint(jax.random.fold_in(key, axis), (), 0, length) for axis, length in enumerate(array.shape)]
    widest = array.shape.index(max(array.shape))
    neighbour = spot[:widest] + [(spot[widest] + 1) % array.shape[widest]] + spot[widest + 1:]
    return array.at[tuple(spot)].set(smallest).at[tuple(neighbour)].set(top_value)


def steps_of(own_key, shape, shards, low, largest):
    loudness, own = 1.0, jax.random.fold_in(own_key, 6)
    for dim, shards_of in shards:
        draws = jnp.exp(jax.random.uniform(jax.random.fold_in(own, dim), (shards_of,), jnp.float32, low / len(shards), largest / len(shards)))
        loudness = loudness * jnp.repeat(draws, shape[dim] // shards_of).reshape([-1 if axis == dim else 1 for axis in range(len(shape))])
    return loudness


def bell_draw(own_key, dims, deviation, most, shards=(), kind=jnp.bfloat16):
    values = deviation * jax.random.normal(own_key, dims, jnp.float32)
    if shards:
        values = values * steps_of(own_key, dims, shards, -0.22, 0.18)
    return jnp.clip(values, -most, most).astype(kind)


def setup_inputs(seed: int = 0) -> dict:
    key_of = jax.random.split(jax.random.key(seed), 4)
    traces = bell_draw(key_of[0], (NT, P_SIZE, NR), 1.0, 6.0, ((0, 4), (2, 8)))
    reflection = bell_draw(key_of[1], (NF, 2, NR, NR), (2 * NR) ** -0.5, 0.0625, ((0, 4), (2, 8)))
    onset = plant(jax.random.randint(key_of[2], (P_SIZE, NR), NT // 4, NT), jax.random.fold_in(key_of[2], 1), NT // 4, NT - 1).astype(jnp.int32)
    return dict(traces=traces, reflection=reflection, onset=onset)


def forward_table(base_band, first_band, band_count, earliest_sample_time, sample_time_count, sampling_interval):
    angular_freq_list = base_band + first_band + jnp.arange(band_count, dtype=jnp.int32)
    sample_moments = earliest_sample_time + jnp.arange(sample_time_count, dtype=jnp.int32)
    phase_angles = (angular_freq_list[:, None] * sample_moments[None, :] % sampling_interval).astype(jnp.float32) * (2.0 * math.pi / sampling_interval)
    factor = 1.0 / math.sqrt(sampling_interval)
    table = jnp.stack([jnp.cos(phase_angles) * factor, -jnp.sin(phase_angles) * factor], axis=1)
    return table.reshape(2 * band_count, sample_time_count).astype(jnp.bfloat16)

def inverse_table(base_band, first_band, band_count, earliest_sample_time, sample_time_count, sampling_interval, bands_total):
    angular_freq_list = base_band + first_band + jnp.arange(band_count, dtype=jnp.int32)
    sample_moments = earliest_sample_time + jnp.arange(sample_time_count, dtype=jnp.int32)
    phase_angles = (sample_moments[:, None] * angular_freq_list[None, :] % sampling_interval).astype(jnp.float32) * (2.0 * math.pi / sampling_interval)
    factor = 1.0 / math.sqrt(bands_total)
    table = jnp.stack([jnp.cos(phase_angles) * factor, -jnp.sin(phase_angles) * factor], axis=2)
    return table.reshape(sample_time_count, 2 * band_count).astype(jnp.bfloat16)

def reference(traces, reflection, onset):
    base_band = NT // 16
    forward = forward_table(base_band, 0, NF, 0, NT, NT)
    spectra = jnp.dot(forward, traces.reshape(NT, P_SIZE * NR), preferred_element_type=jnp.float32)
    spectra = spectra.astype(jnp.bfloat16).reshape(NF, 2, P_SIZE, NR)

    def respond(operands):
        spectrum, matrix = operands
        product = jnp.dot(spectrum.reshape(2 * P_SIZE, NR), matrix.reshape(2 * NR, NR).T, preferred_element_type=jnp.float32)
        product = product.reshape(2, P_SIZE, 2, NR)
        return jnp.stack([product[0, :, 0] - product[1, :, 1], product[1, :, 0] + product[0, :, 1]]).astype(jnp.bfloat16)
    response = lax.map(respond, (spectra, reflection))
    response_rows = response.reshape(2 * NF, P_SIZE * NR)
    tile_row_group = NT // N_FREQ

    def window(block_index):
        earliest_sample_time = block_index * tile_row_group
        inverse = inverse_table(base_band, 0, NF, earliest_sample_time, tile_row_group, NT, NF)
        wavelet_trace = jnp.dot(inverse, response_rows, preferred_element_type=jnp.float32).reshape(tile_row_group, P_SIZE, NR)
        sample_moments = earliest_sample_time + jnp.arange(tile_row_group, dtype=jnp.int32)
        return jnp.where(sample_moments[:, None, None] < onset[None], wavelet_trace, 0.0).astype(jnp.bfloat16)
    windowed = lax.map(window, jnp.arange(N_FREQ, dtype=jnp.int32))
    return windowed.reshape(NT, P_SIZE, NR)
```

```python
import functools
import math

import jax
import jax.numpy as jnp
from jax import lax
from jax.experimental import pallas as pl
from jax.experimental.pallas import tpu as pltpu
from jax.sharding import PartitionSpec as P

ROWS = 16
CHUNKS = 2
F_TIMES = 128
I_TIMES = 64
R_ROWS = 128
VMEM = 56 * 1024 * 1024


def phases(bands, times, samples):
    return (bands * times % samples).astype(jnp.float32) * (2.0 * math.pi / samples)


def tables(per_device, freq_devices, local_times):
    me = lax.axis_index("freq")
    samples = local_times * freq_devices
    owners = me ^ jnp.arange(freq_devices, dtype=jnp.int32)
    bands = samples // 16 + (owners[:, None] * per_device + jnp.arange(per_device, dtype=jnp.int32)).reshape(-1)
    times = me * local_times + jnp.arange(local_times, dtype=jnp.int32)
    rows = phases(bands[:, None], times[None, :], samples)
    factor = 1.0 / math.sqrt(samples)
    forward = jnp.stack([jnp.cos(rows) * factor, -jnp.sin(rows) * factor], axis=1)
    columns = phases(bands[None, :], times[:, None], samples)
    factor = 1.0 / math.sqrt(per_device * freq_devices)
    inverse = jnp.stack([jnp.cos(columns) * factor, -jnp.sin(columns) * factor], axis=2)
    return (
        forward.reshape(-1, local_times).astype(jnp.bfloat16),
        inverse.reshape(local_times, -1).astype(jnp.bfloat16),
    )


def forward_kernel(table_ref, traces_ref, *refs):
    outs, (spread, total) = refs[:-2], refs[-2:]
    block, step = pl.program_id(0), pl.program_id(1)
    times, rows, width = traces_ref.shape
    lanes = times * rows
    count = table_ref.shape[0]

    @pl.when(block == 0)
    def _():
        lane = lax.broadcasted_iota(jnp.int32, (times, lanes), 1)
        row = lax.broadcasted_iota(jnp.int32, (times, lanes), 0)
        repeat = jnp.where(lane // rows == row, 1.0, 0.0).astype(jnp.bfloat16)
        wide = jnp.dot(table_ref[...], repeat, preferred_element_type=jnp.float32)
        lane = lax.broadcasted_iota(jnp.int32, (rows, lanes), 1)
        row = lax.broadcasted_iota(jnp.int32, (rows, lanes), 0)
        own = lane % rows == row
        for i in range(count):
            spread[step, pl.ds(i * rows, rows), :] = jnp.where(own, wide[i : i + 1], 0.0).astype(jnp.bfloat16)

    part = jnp.dot(
        spread[step], traces_ref[...].reshape(lanes, width), preferred_element_type=jnp.float32
    )

    @pl.when(step == 0)
    def _():
        total[...] = part

    @pl.when(step > 0)
    def _():
        total[...] += part

    @pl.when(step == pl.num_programs(1) - 1)
    def _():
        share = count * rows // len(outs)
        for i, out in enumerate(outs):
            out[...] = total[pl.ds(i * share, share), :].reshape(out.shape).astype(out.dtype)


def forward(table, traces, first, focal, per_device, freq_devices):
    local_times, _, width = traces.shape
    count = table.shape[0]
    times = min(F_TIMES, local_times)
    steps = local_times // times
    shape = (per_device, 2, focal, width)
    return pl.pallas_call(
        forward_kernel,
        grid=(focal // ROWS, steps),
        in_specs=[
            pl.BlockSpec((count, times), lambda p, t: (0, t)),
            pl.BlockSpec((times, ROWS, width), lambda p, t: (t, first // ROWS + p, 0)),
        ],
        out_specs=[
            pl.BlockSpec((per_device, 2, ROWS, width), lambda p, t: (0, 0, p, 0)) for _ in range(freq_devices)
        ],
        out_shape=[
            jax.ShapeDtypeStruct(shape, jnp.float32 if i == 0 else jnp.bfloat16) for i in range(freq_devices)
        ],
        scratch_shapes=[
            pltpu.VMEM((steps, count * ROWS, times * ROWS), jnp.bfloat16),
            pltpu.VMEM((count * ROWS, width), jnp.float32),
        ],
        compiler_params=pltpu.CompilerParams(vmem_limit_bytes=VMEM),
        cost_estimate=pl.CostEstimate(
            flops=2 * count * ROWS * local_times * focal * width,
            bytes_accessed=2 * local_times * focal * width,
            transcendentals=0,
        ),
        name="forward",
    )(table, traces)


def response_kernel(place_ref, reflection_ref, *refs):
    pieces, (out, spectra) = refs[:-2], refs[-2:]
    band, step = pl.program_id(0), pl.program_id(1)
    _, _, rows, sources = reflection_ref.shape
    _, _, focal, width = pieces[0].shape

    @pl.when((band == 0) & (step == 0))
    def _():
        for i, piece in enumerate(pieces):
            start = pl.multiple_of(place_ref[i] * width, width)
            spectra[:, :, pl.ds(start, width)] = piece[...].reshape(-1, 2 * focal, width)

    product = lax.dot_general(
        spectra[band],
        reflection_ref[...].reshape(2 * rows, sources),
        (((1,), (1,)), ((), ())),
        preferred_element_type=jnp.float32,
    )
    out[0, 0] = (product[:focal, :rows] - product[focal:, rows:]).astype(out.dtype)
    out[0, 1] = (product[focal:, :rows] + product[:focal, rows:]).astype(out.dtype)


def respond(reflection, places, pieces):
    per_device, _, width, sources = reflection.shape
    focal = pieces[0].shape[2]
    rows = min(R_ROWS, width)
    return pl.pallas_call(
        response_kernel,
        grid=(per_device, width // rows),
        in_specs=[
            pl.BlockSpec(memory_space=pltpu.SMEM),
            pl.BlockSpec((1, 2, rows, sources), lambda k, r: (k, 0, r, 0)),
        ]
        + [pl.BlockSpec(p.shape, lambda k, r: (0, 0, 0, 0), pipeline_mode=pl.Buffered(1)) for p in pieces],
        out_specs=pl.BlockSpec((1, 2, focal, rows), lambda k, r: (k, 0, 0, r)),
        out_shape=jax.ShapeDtypeStruct((per_device, 2, focal, width), jnp.bfloat16),
        scratch_shapes=[pltpu.VMEM((per_device, 2 * focal, sources), jnp.bfloat16)],
        compiler_params=pltpu.CompilerParams(vmem_limit_bytes=VMEM),
        cost_estimate=pl.CostEstimate(
            flops=8 * per_device * focal * width * sources,
            bytes_accessed=4 * per_device * width * sources,
            transcendentals=0,
        ),
        name="respond",
    )(places, reflection, *pieces)


def inverse_kernel(has_before, table_ref, onset_ref, *refs):
    pieces, (out, spread, weights) = refs[: -3 - has_before], refs[-3:]
    block, step = pl.program_id(0), pl.program_id(1)
    times, rows, width = out.shape
    count = table_ref.shape[1]
    lanes = count * rows

    @pl.when(block == 0)
    def _():
        lane = lax.broadcasted_iota(jnp.int32, (count, lanes), 1)
        row = lax.broadcasted_iota(jnp.int32, (count, lanes), 0)
        repeat = jnp.where(lane // rows == row, 1.0, 0.0).astype(jnp.bfloat16)
        wide = jnp.dot(table_ref[...], repeat, preferred_element_type=jnp.float32)
        lane = lax.broadcasted_iota(jnp.int32, (rows, lanes), 1)
        row = lax.broadcasted_iota(jnp.int32, (rows, lanes), 0)
        own = lane % rows == row
        for i in range(times):
            spread[step, pl.ds(i * rows, rows), :] = jnp.where(own, wide[i : i + 1], 0.0).astype(jnp.bfloat16)

    @pl.when(step == 0)
    def _():
        share = lanes // len(pieces)
        for i, piece in enumerate(pieces):
            weights[pl.ds(i * share, share), :] = piece[...].reshape(share, width)

    signal = jnp.dot(spread[step], weights[...], preferred_element_type=jnp.float32)
    signal = signal.reshape(times, rows, width)
    first = (lax.axis_index("freq") * pl.num_programs(1) + step) * times
    moment = first + lax.broadcasted_iota(jnp.int32, (times, 1, 1), 0)
    out[...] = jnp.where(moment < onset_ref[...][None], signal, 0.0).astype(out.dtype)


def invert(table, onset, pieces, before, first, shape):
    local_times, _, width = shape
    focal = pieces[0].shape[2]
    count = table.shape[1]
    times = min(I_TIMES, local_times)
    steps = local_times // times
    has_before = before is not None
    operands = [table, onset, *pieces] + ([before] if has_before else [])
    return pl.pallas_call(
        functools.partial(inverse_kernel, has_before),
        grid=(focal // ROWS, steps),
        in_specs=[
            pl.BlockSpec((times, count), lambda p, t: (t, 0)),
            pl.BlockSpec((ROWS, width), lambda p, t: (first // ROWS + p, 0)),
        ]
        + [pl.BlockSpec((p.shape[0], 2, ROWS, width), lambda p, t: (0, 0, p, 0)) for p in pieces]
        + ([pl.BlockSpec(memory_space=pl.ANY)] if has_before else []),
        out_specs=pl.BlockSpec((times, ROWS, width), lambda p, t: (t, first // ROWS + p, 0)),
        out_shape=jax.ShapeDtypeStruct(shape, jnp.bfloat16),
        scratch_shapes=[
            pltpu.VMEM((steps, times * ROWS, count * ROWS), jnp.bfloat16),
            pltpu.VMEM((count * ROWS, width), jnp.bfloat16),
        ],
        input_output_aliases={len(operands) - 1: 0} if has_before else {},
        compiler_params=pltpu.CompilerParams(vmem_limit_bytes=VMEM),
        cost_estimate=pl.CostEstimate(
            flops=2 * count * ROWS * local_times * focal * width,
            bytes_accessed=2 * local_times * focal * width,
            transcendentals=0,
        ),
        name="invert",
    )(*operands)


def swap(array, axis, mask):
    return lax.ppermute(array, axis, [(i, i ^ mask) for i in range(lax.axis_size(axis))])


def on_device(traces, reflection, onset):
    local_times, focal_count, _ = traces.shape
    freq_devices, mat_devices = lax.axis_size("freq"), lax.axis_size("mat")
    per_device = reflection.shape[0]
    forward_table, inverse_table = tables(per_device, freq_devices, local_times)
    focal = focal_count // CHUNKS

    masks = list(range(0, mat_devices, 2))
    places = lax.axis_index("mat") ^ jnp.array([m ^ c for m in masks for c in (0, 1)], jnp.int32)

    parts = [
        forward(forward_table, traces, i * focal, focal, per_device, freq_devices) for i in range(CHUNKS)
    ]
    responses = []
    for part in parts:
        spectra = part[0]
        for mask in range(1, freq_devices):
            spectra = spectra + swap(part[mask], "freq", mask).astype(jnp.float32)
        spectra = spectra.astype(jnp.bfloat16)
        pieces = []
        for mask in masks:
            piece = swap(spectra, "mat", mask) if mask else spectra
            pieces += [piece, swap(piece, "mat", 1)]
        response = respond(reflection, places, pieces)
        responses.append([response] + [swap(response, "freq", mask) for mask in range(1, freq_devices)])
    windowed = None
    for i, pieces in enumerate(responses):
        windowed = invert(inverse_table, onset, pieces, windowed, i * focal, traces.shape)
    return windowed


def solution(mesh):
    placed = (P("freq", None, "mat"), P("freq", None, "mat", None), P(None, "mat"))
    return jax.shard_map(
        on_device, mesh=mesh, in_specs=placed, out_specs=P("freq", None, "mat"), check_vma=False
    )
```

```python
import functools
import math

import jax
import jax.numpy as jnp
from jax import lax
from jax.experimental import pallas as pl
from jax.experimental.pallas import tpu as pltpu
from jax.sharding import PartitionSpec as P

ROWS = 16
CHUNKS = 2
F_TIMES = 128
F_SLOTS = 3
I_TIMES = 128
I_SLOTS = 3
R_ROWS = 128
R_FLIGHT = 3
MIB = 1024 * 1024
F_VMEM = 40 * MIB
R_VMEM = 47 * MIB
I_VMEM = 24 * MIB
S_VMEM = 40 * MIB


def phases(bands, times, samples):
    return (bands * times % samples).astype(jnp.float32) * (2.0 * math.pi / samples)


def tables(per_device, freq_devices, local_times):
    me = lax.axis_index("freq")
    samples = local_times * freq_devices
    owners = me ^ jnp.arange(freq_devices, dtype=jnp.int32)
    bands = samples // 16 + (owners[:, None] * per_device + jnp.arange(per_device, dtype=jnp.int32)).reshape(-1)
    times = me * local_times + jnp.arange(local_times, dtype=jnp.int32)
    rows = phases(bands[:, None], times[None, :], samples)
    factor = 1.0 / math.sqrt(samples)
    forward = jnp.stack([jnp.cos(rows) * factor, -jnp.sin(rows) * factor], axis=1)
    columns = phases(bands[None, :], times[:, None], samples)
    factor = 1.0 / math.sqrt(per_device * freq_devices)
    inverse = jnp.stack([jnp.cos(columns) * factor, -jnp.sin(columns) * factor], axis=2)
    return (
        forward.reshape(-1, local_times).astype(jnp.bfloat16),
        inverse.reshape(local_times, -1).astype(jnp.bfloat16),
    )


def expand(table, rows):
    count = table.shape[1]
    lane = lax.broadcasted_iota(jnp.int32, (count, count * rows), 1)
    row = lax.broadcasted_iota(jnp.int32, (count, count * rows), 0)
    repeat = jnp.where(lane // rows == row, 1.0, 0.0).astype(jnp.bfloat16)
    return jnp.dot(table, repeat, preferred_element_type=jnp.float32)


def spread_rows(store, wide):
    lane = lax.broadcasted_iota(jnp.int32, (ROWS, wide.shape[1]), 1)
    row = lax.broadcasted_iota(jnp.int32, (ROWS, wide.shape[1]), 0)
    own = lane % ROWS == row
    for i in range(wide.shape[0]):
        store(i, jnp.where(own, wide[i : i + 1], 0.0).astype(jnp.bfloat16))


def forward_kernel(first, focal, table_ref, traces_ref, *refs):
    *outs, spread, total, slots, sems = refs
    depth, times, rows, width = slots.shape
    steps = spread.shape[0]
    count = steps * (focal // rows)

    def fetch(i):
        slot = lax.rem(i, depth)
        source = traces_ref.at[
            pl.ds(lax.rem(i, steps) * times, times), pl.ds(first + i // steps * rows, rows), :
        ]
        return pltpu.make_async_copy(source, slots.at[slot], sems.at[slot])

    for i in range(min(depth - 1, count)):
        fetch(jnp.int32(i)).start()

    for step in range(steps):

        def store(i, block, step=step):
            spread[step, pl.ds(i * rows, rows), :] = block

        spread_rows(store, expand(table_ref[:, pl.ds(step * times, times)], rows))

    @pl.loop(0, count)
    def _(i):
        step = lax.rem(i, steps)

        @pl.when(i + depth - 1 < count)
        def _():
            fetch(i + depth - 1).start()

        fetch(i).wait()
        block = slots[lax.rem(i, depth)].reshape(times * rows, width)
        part = jnp.dot(spread[step], block, preferred_element_type=jnp.float32)

        @pl.when(step == 0)
        def _():
            total[...] = part

        @pl.when(step > 0)
        def _():
            total[...] += part

        @pl.when(step == steps - 1)
        def _():
            share = total.shape[0] // len(outs)
            place = pl.ds(pl.multiple_of(i // steps * rows, rows), rows)
            for j, out in enumerate(outs):
                value = total[pl.ds(j * share, share), :].reshape(*out.shape[:2], rows, width)
                out[:, :, place, :] = value.astype(out.dtype)


def forward(table, traces, first, focal, per_device, freq_devices):
    local_times, _, width = traces.shape
    times = min(F_TIMES, local_times)
    steps = local_times // times
    count = 2 * per_device * freq_devices
    shape = (per_device, 2, focal, width)
    whole = pl.BlockSpec(memory_space=pltpu.VMEM)
    return pl.pallas_call(
        functools.partial(forward_kernel, first, focal),
        in_specs=[whole, pl.BlockSpec(memory_space=pl.ANY)],
        out_specs=[whole] * freq_devices,
        out_shape=[jax.ShapeDtypeStruct(shape, jnp.float32 if i == 0 else jnp.bfloat16) for i in range(freq_devices)],
        scratch_shapes=[
            pltpu.VMEM((steps, count * ROWS, times * ROWS), jnp.bfloat16),
            pltpu.VMEM((count * ROWS, width), jnp.float32),
            pltpu.VMEM((F_SLOTS, times, ROWS, width), jnp.bfloat16),
            pltpu.SemaphoreType.DMA((F_SLOTS,)),
        ],
        compiler_params=pltpu.CompilerParams(vmem_limit_bytes=F_VMEM),
        cost_estimate=pl.CostEstimate(
            flops=2 * count * ROWS * local_times * focal * width,
            bytes_accessed=2 * local_times * focal * width,
            transcendentals=0,
        ),
        name="forward",
    )(table, traces)


def response_kernel(place_ref, reflection_ref, own_ref, other_ref, out, spectra, slots, sems):
    bands, cuts, _, rows, sources = slots.shape
    _, _, _, focal, width = own_ref.shape

    def fetch(band, cut):
        source = reflection_ref.at[band, :, pl.ds(cut * rows, rows), :]
        return pltpu.make_async_copy(source, slots.at[band, cut], sems.at[band, cut])

    order = [(band, cut) for band in range(bands) for cut in range(cuts)]
    for block in order[:R_FLIGHT]:
        fetch(*block).start()
    for i in range(2 * own_ref.shape[0]):
        start = pl.multiple_of(place_ref[i] * width, width)
        for band in range(bands):
            piece = (own_ref, other_ref)[i % 2][i // 2, band].reshape(2 * focal, width)
            spectra[band, pl.ds(start, width), :] = piece.T
    for i, (band, cut) in enumerate(order):
        fetch(band, cut).wait()
        for block in order[i + R_FLIGHT : i + R_FLIGHT + 1]:
            fetch(*block).start()
        product = jnp.dot(
            slots[band, cut].reshape(2 * rows, sources), spectra[band], preferred_element_type=jnp.float32
        ).T
        place = pl.ds(cut * rows, rows)
        out[band, 0, :, place] = (product[:focal, :rows] - product[focal:, rows:]).astype(out.dtype)
        out[band, 1, :, place] = (product[focal:, :rows] + product[:focal, rows:]).astype(out.dtype)


def respond(reflection, places, own, other):
    per_device, _, width, sources = reflection.shape
    focal = own.shape[3]
    cuts = max(1, width // R_ROWS)
    whole = pl.BlockSpec(memory_space=pltpu.VMEM)
    return pl.pallas_call(
        response_kernel,
        in_specs=[pl.BlockSpec(memory_space=pltpu.SMEM), pl.BlockSpec(memory_space=pl.ANY), whole, whole],
        out_specs=whole,
        out_shape=jax.ShapeDtypeStruct((per_device, 2, focal, width), jnp.bfloat16),
        scratch_shapes=[
            pltpu.VMEM((per_device, sources, 2 * focal), jnp.bfloat16),
            pltpu.VMEM((per_device, cuts, 2, width // cuts, sources), jnp.bfloat16),
            pltpu.SemaphoreType.DMA((per_device, cuts)),
        ],
        compiler_params=pltpu.CompilerParams(vmem_limit_bytes=R_VMEM),
        cost_estimate=pl.CostEstimate(
            flops=8 * per_device * focal * width * sources,
            bytes_accessed=4 * per_device * width * sources,
            transcendentals=0,
        ),
        name="respond",
    )(places, reflection, own, other)


def inverse_kernel(first, has_before, table_ref, onset_ref, *refs):
    pieces, (out, spread, weights, slots, sems) = refs[: -5 - has_before], refs[-5:]
    depth, times, rows, width = slots.shape
    focal = pieces[0].shape[2]
    local_times = out.shape[0]
    steps = local_times // times
    count = steps * (focal // rows)
    share = weights.shape[0] // len(pieces)
    begin = lax.axis_index("freq") * local_times

    def store(i, block):
        spread[pl.ds(i * rows, rows), :] = block

    spread_rows(store, expand(table_ref[...], rows))

    def send(i):
        slot = lax.rem(i, depth)
        target = out.at[pl.ds(lax.rem(i, steps) * times, times), pl.ds(first + i // steps * rows, rows), :]
        return pltpu.make_async_copy(slots.at[slot], target, sems.at[slot])

    @pl.loop(0, count)
    def _(i):
        step = lax.rem(i, steps)
        slot = lax.rem(i, depth)
        place = pl.ds(pl.multiple_of(i // steps * rows, rows), rows)

        @pl.when(i >= depth)
        def _():
            send(i - depth).wait()

        @pl.when(step == 0)
        def _():
            for j, piece in enumerate(pieces):
                weights[pl.ds(j * share, share), :] = piece[:, :, place, :].reshape(share, width)

        lines = pl.ds(pl.multiple_of(step * times * rows, times * rows), times * rows)
        signal = jnp.dot(spread[lines, :], weights[...], preferred_element_type=jnp.float32)
        signal = signal.reshape(times, rows, width)
        moment = begin + step * times + lax.broadcasted_iota(jnp.int32, (times, 1, 1), 0)
        onset = onset_ref[pl.ds(pl.multiple_of(first + i // steps * rows, rows), rows), :]
        slots[slot] = jnp.where(moment < onset[None], signal, 0.0).astype(out.dtype)
        send(i).start()

    for i in range(max(0, count - depth), count):
        send(jnp.int32(i)).wait()


def invert(table, onset, pieces, before, first, shape):
    local_times, _, width = shape
    focal = pieces[0].shape[2]
    times = min(I_TIMES, local_times)
    has_before = before is not None
    operands = [table, onset, *pieces] + ([before] if has_before else [])
    whole = pl.BlockSpec(memory_space=pltpu.VMEM)
    anywhere = pl.BlockSpec(memory_space=pl.ANY)
    return pl.pallas_call(
        functools.partial(inverse_kernel, first, has_before),
        in_specs=[whole] * (2 + len(pieces)) + [anywhere] * has_before,
        out_specs=anywhere,
        out_shape=jax.ShapeDtypeStruct(shape, jnp.bfloat16),
        scratch_shapes=[
            pltpu.VMEM((local_times * ROWS, table.shape[1] * ROWS), jnp.bfloat16),
            pltpu.VMEM((table.shape[1] * ROWS, width), jnp.bfloat16),
            pltpu.VMEM((I_SLOTS, times, ROWS, width), jnp.bfloat16),
            pltpu.SemaphoreType.DMA((I_SLOTS,)),
        ],
        input_output_aliases={len(operands) - 1: 0} if has_before else {},
        compiler_params=pltpu.CompilerParams(vmem_limit_bytes=I_VMEM),
        cost_estimate=pl.CostEstimate(
            flops=2 * table.shape[1] * ROWS * local_times * focal * width,
            bytes_accessed=2 * local_times * focal * width,
            transcendentals=0,
        ),
        name="invert",
    )(*operands)


def stack_kernel(*refs):
    *pieces, _, out = refs
    for i, piece in enumerate(pieces):
        out[i] = piece[...]


def stack(pieces, earlier):
    whole = pl.BlockSpec(memory_space=pltpu.VMEM)
    return pl.pallas_call(
        stack_kernel,
        in_specs=[whole] * len(pieces) + [pl.BlockSpec(memory_space=pl.ANY)],
        out_specs=whole,
        out_shape=jax.ShapeDtypeStruct((len(pieces), *pieces[0].shape), pieces[0].dtype),
        compiler_params=pltpu.CompilerParams(vmem_limit_bytes=S_VMEM),
        name="stack",
    )(*pieces, earlier)


def swap(array, axis, mask):
    return lax.ppermute(array, axis, [(i, i ^ mask) for i in range(lax.axis_size(axis))])


def on_device(traces, reflection, onset):
    local_times, focal_count, _ = traces.shape
    freq_devices, mat_devices = lax.axis_size("freq"), lax.axis_size("mat")
    per_device = reflection.shape[0]
    forward_table, inverse_table = tables(per_device, freq_devices, local_times)
    focal = focal_count // CHUNKS

    masks = list(range(0, mat_devices, 2))
    places = lax.axis_index("mat") ^ jnp.array([m ^ c for m in masks for c in (0, 1)], jnp.int32)

    parts = [
        forward(forward_table, traces, i * focal, focal, per_device, freq_devices) for i in range(CHUNKS)
    ]
    spectra = []
    for part in parts:
        total = part[0]
        for mask in range(1, freq_devices):
            total = total + swap(part[mask], "freq", mask).astype(jnp.float32)
        spectra.append(total.astype(jnp.bfloat16))
    gathered = [[swap(own, "mat", mask) if mask else own for mask in masks] for own in spectra]
    responses = []
    for i, pieces in enumerate(gathered):
        own = stack(pieces, responses[-1][0] if responses else spectra[-1])
        response = respond(reflection, places, own, swap(own, "mat", 1))
        responses.append([response] + [swap(response, "freq", mask) for mask in range(1, freq_devices)])
    windowed = None
    for i, pieces in enumerate(responses):
        windowed = invert(inverse_table, onset, pieces, windowed, i * focal, traces.shape)
    return windowed


def solution(mesh):
    placed = (P("freq", None, "mat"), P("freq", None, "mat", None), P(None, "mat"))
    return jax.shard_map(
        on_device, mesh=mesh, in_specs=placed, out_specs=P("freq", None, "mat"), check_vma=False
    )
```

```python
import functools
import math

import jax
import jax.numpy as jnp
from jax import lax
from jax.experimental import pallas as pl
from jax.experimental.pallas import tpu as pltpu
from jax.sharding import PartitionSpec as P

ROWS = 16
CHUNKS = 2
F_TIMES = 256
F_SLOTS = 3
I_TIMES = 128
I_SLOTS = 3
MIB = 1024 * 1024
F_VMEM = 40 * MIB
R_VMEM = 12 * MIB
I_VMEM = 20 * MIB
S_VMEM = 16 * MIB
L_VMEM = 32 * MIB


def phases(bands, times, samples):
    return (bands * times % samples).astype(jnp.float32) * (2.0 * math.pi / samples)


def tables(per_device, freq_devices, local_times):
    me = lax.axis_index("freq")
    samples = local_times * freq_devices
    owners = me ^ jnp.arange(freq_devices, dtype=jnp.int32)
    bands = samples // 16 + (owners[:, None] * per_device + jnp.arange(per_device, dtype=jnp.int32)).reshape(-1)
    times = me * local_times + jnp.arange(local_times, dtype=jnp.int32)
    angles = phases(bands[:, None], times[None, :], samples)
    parts = jnp.stack([jnp.cos(angles), -jnp.sin(angles)], axis=1).reshape(-1, local_times)
    factors = (1.0 / math.sqrt(samples), 1.0 / math.sqrt(per_device * freq_devices))
    return jnp.stack([parts * factor for factor in factors]).astype(jnp.bfloat16)


def repeats(count):
    lane = lax.broadcasted_iota(jnp.int32, (count, count * ROWS), 1)
    row = lax.broadcasted_iota(jnp.int32, (count, count * ROWS), 0)
    return jnp.where(lane // ROWS == row, 1.0, 0.0).astype(jnp.bfloat16)


def spread_rows(store, wide):
    lane = lax.broadcasted_iota(jnp.int32, (ROWS, wide.shape[1]), 1)
    row = lax.broadcasted_iota(jnp.int32, (ROWS, wide.shape[1]), 0)
    own = lane % ROWS == row
    for i in range(wide.shape[0]):
        store(i, jnp.where(own, wide[i : i + 1], 0.0).astype(jnp.bfloat16))


def forward_kernel(first, focal, table_ref, traces_ref, *refs):
    *outs, spread, total, slots, sems = refs
    depth, times, rows, width = slots.shape
    steps = spread.shape[0]
    count = steps * (focal // rows)

    def fetch(i):
        slot = lax.rem(i, depth)
        source = traces_ref.at[
            pl.ds(lax.rem(i, steps) * times, times), pl.ds(first + i // steps * rows, rows), :
        ]
        return pltpu.make_async_copy(source, slots.at[slot], sems.at[slot])

    for i in range(min(depth - 1, count)):
        fetch(jnp.int32(i)).start()

    for step in range(steps):

        def store(i, block, step=step):
            spread[step, pl.ds(i * rows, rows), :] = block

        some = table_ref[0, :, pl.ds(step * times, times)]
        spread_rows(store, jnp.dot(some, repeats(times), preferred_element_type=jnp.float32))

    @pl.loop(0, count)
    def _(i):
        step = lax.rem(i, steps)

        @pl.when(i + depth - 1 < count)
        def _():
            fetch(i + depth - 1).start()

        fetch(i).wait()
        block = slots[lax.rem(i, depth)].reshape(times * rows, width)
        part = jnp.dot(spread[step], block, preferred_element_type=jnp.float32)

        @pl.when(step == 0)
        def _():
            total[...] = part

        @pl.when(step > 0)
        def _():
            total[...] += part

        @pl.when(step == steps - 1)
        def _():
            share = total.shape[0] // len(outs)
            place = pl.ds(pl.multiple_of(i // steps * rows, rows), rows)
            for j, out in enumerate(outs):
                value = total[pl.ds(j * share, share), :].reshape(*out.shape[:2], rows, width)
                out[:, :, place, :] = value.astype(out.dtype)


def forward(table, traces, first, focal, per_device, freq_devices):
    local_times, _, width = traces.shape
    times = min(F_TIMES, local_times)
    steps = local_times // times
    count = 2 * per_device * freq_devices
    shape = (per_device, 2, focal, width)
    whole = pl.BlockSpec(memory_space=pltpu.VMEM)
    return pl.pallas_call(
        functools.partial(forward_kernel, first, focal),
        in_specs=[whole, pl.BlockSpec(memory_space=pl.ANY)],
        out_specs=[whole] * freq_devices,
        out_shape=[jax.ShapeDtypeStruct(shape, jnp.float32 if i == 0 else jnp.bfloat16) for i in range(freq_devices)],
        scratch_shapes=[
            pltpu.VMEM((steps, count * ROWS, times * ROWS), jnp.bfloat16),
            pltpu.VMEM((count * ROWS, width), jnp.float32),
            pltpu.VMEM((F_SLOTS, times, ROWS, width), jnp.bfloat16),
            pltpu.SemaphoreType.DMA((F_SLOTS,)),
        ],
        compiler_params=pltpu.CompilerParams(vmem_limit_bytes=F_VMEM),
        cost_estimate=pl.CostEstimate(
            flops=2 * count * ROWS * local_times * focal * width,
            bytes_accessed=2 * local_times * focal * width,
            transcendentals=0,
        ),
        name="forward",
    )(table, traces)


def load_kernel(reflection_ref, *refs):
    out, sems = refs[-2:]

    def fetch(i):
        return pltpu.make_async_copy(reflection_ref.at[i], out.at[i], sems.at[i])

    for i in range(out.shape[0]):
        fetch(i).start()
    for i in range(out.shape[0]):
        fetch(i).wait()


def load(reflection, earlier):
    return pl.pallas_call(
        load_kernel,
        in_specs=[pl.BlockSpec(memory_space=pl.ANY)] * (1 + len(earlier)),
        out_specs=pl.BlockSpec(memory_space=pltpu.VMEM),
        out_shape=jax.ShapeDtypeStruct(reflection.shape, reflection.dtype),
        scratch_shapes=[pltpu.SemaphoreType.DMA((reflection.shape[0],))],
        compiler_params=pltpu.CompilerParams(vmem_limit_bytes=L_VMEM),
        name="load",
    )(reflection, *earlier)


def response_kernel(masks, reflection_ref, *refs):
    out, spectra = refs[-2:]
    bands, _, rows, sources = reflection_ref.shape
    _, _, _, focal, width = refs[0].shape
    me = lax.axis_index("mat")
    for pieces, origins in zip(refs, masks):
        for i, mask in enumerate(origins):
            start = pl.multiple_of((me ^ mask) * width, width)
            spectra[:, :, pl.ds(start, width)] = pieces[i].reshape(bands, 2 * focal, width)
    for band in range(bands):
        product = lax.dot_general(
            reflection_ref[band].reshape(2 * rows, sources),
            spectra[band],
            (((1,), (1,)), ((), ())),
            preferred_element_type=jnp.float32,
        ).T
        out[band, 0] = (product[:focal, :rows] - product[focal:, rows:]).astype(out.dtype)
        out[band, 1] = (product[focal:, :rows] + product[:focal, rows:]).astype(out.dtype)


def respond(reflection, pieces, masks, earlier):
    per_device, _, rows, sources = reflection.shape
    focal, width = pieces[0].shape[3:]
    whole = pl.BlockSpec(memory_space=pltpu.VMEM)
    return pl.pallas_call(
        functools.partial(response_kernel, masks),
        in_specs=[whole] * (1 + len(pieces)) + [pl.BlockSpec(memory_space=pl.ANY)] * len(earlier),
        out_specs=whole,
        out_shape=jax.ShapeDtypeStruct((per_device, 2, focal, rows), jnp.bfloat16),
        scratch_shapes=[pltpu.VMEM((per_device, 2 * focal, sources), jnp.bfloat16)],
        compiler_params=pltpu.CompilerParams(vmem_limit_bytes=R_VMEM),
        cost_estimate=pl.CostEstimate(flops=0, bytes_accessed=1024, transcendentals=0),
        name="respond",
    )(reflection, *pieces, *earlier)


def spread_kernel(table_ref, out):
    def store(i, block):
        out[pl.ds(i * ROWS, ROWS), :] = block

    table = table_ref[1]
    wide = lax.dot_general(
        table, repeats(table.shape[0]), (((0,), (0,)), ((), ())), preferred_element_type=jnp.float32
    )
    spread_rows(store, wide)


def spread(table):
    _, count, times = table.shape
    whole = pl.BlockSpec(memory_space=pltpu.VMEM)
    return pl.pallas_call(
        spread_kernel,
        in_specs=[whole],
        out_specs=whole,
        out_shape=jax.ShapeDtypeStruct((times * ROWS, count * ROWS), jnp.bfloat16),
        compiler_params=pltpu.CompilerParams(vmem_limit_bytes=S_VMEM),
        cost_estimate=pl.CostEstimate(flops=0, bytes_accessed=2 * times * ROWS * count * ROWS, transcendentals=0),
        name="spread",
    )(table)


def inverse_kernel(first, has_before, spread, onset_ref, *refs):
    pieces, (out, weights, slots, sems) = refs[: -4 - has_before], refs[-4:]
    depth, times, rows, width = slots.shape
    focal = pieces[0].shape[2]
    local_times = out.shape[0]
    steps = local_times // times
    count = steps * (focal // rows)
    share = weights.shape[0] // len(pieces)
    begin = lax.axis_index("freq") * local_times

    def send(i):
        slot = lax.rem(i, depth)
        target = out.at[pl.ds(lax.rem(i, steps) * times, times), pl.ds(first + i // steps * rows, rows), :]
        return pltpu.make_async_copy(slots.at[slot], target, sems.at[slot])

    @pl.loop(0, count)
    def _(i):
        step = lax.rem(i, steps)
        slot = lax.rem(i, depth)
        place = pl.ds(pl.multiple_of(i // steps * rows, rows), rows)

        @pl.when(i >= depth)
        def _():
            send(i - depth).wait()

        @pl.when(step == 0)
        def _():
            for j, piece in enumerate(pieces):
                weights[pl.ds(j * share, share), :] = piece[:, :, place, :].reshape(share, width)

        lines = pl.ds(pl.multiple_of(step * times * rows, times * rows), times * rows)
        signal = jnp.dot(spread[lines, :], weights[...], preferred_element_type=jnp.float32)
        signal = signal.reshape(times, rows, width)
        moment = begin + step * times + lax.broadcasted_iota(jnp.int32, (times, 1, 1), 0)
        onset = onset_ref[pl.ds(pl.multiple_of(first + i // steps * rows, rows), rows), :]
        slots[slot] = jnp.where(moment < onset[None], signal, 0.0).astype(out.dtype)
        send(i).start()

    for i in range(max(0, count - depth), count):
        send(jnp.int32(i)).wait()


def invert(table, onset, pieces, before, first, shape):
    local_times, _, width = shape
    focal = pieces[0].shape[2]
    times = min(I_TIMES, local_times)
    has_before = before is not None
    operands = [table, onset, *pieces] + ([before] if has_before else [])
    whole = pl.BlockSpec(memory_space=pltpu.VMEM)
    anywhere = pl.BlockSpec(memory_space=pl.ANY)
    return pl.pallas_call(
        functools.partial(inverse_kernel, first, has_before),
        in_specs=[whole] * (2 + len(pieces)) + [anywhere] * has_before,
        out_specs=anywhere,
        out_shape=jax.ShapeDtypeStruct(shape, jnp.bfloat16),
        scratch_shapes=[
            pltpu.VMEM((table.shape[1], width), jnp.bfloat16),
            pltpu.VMEM((I_SLOTS, times, ROWS, width), jnp.bfloat16),
            pltpu.SemaphoreType.DMA((I_SLOTS,)),
        ],
        input_output_aliases={len(operands) - 1: 0} if has_before else {},
        compiler_params=pltpu.CompilerParams(vmem_limit_bytes=I_VMEM),
        cost_estimate=pl.CostEstimate(
            flops=2 * table.shape[1] * local_times * focal * width,
            bytes_accessed=2 * local_times * focal * width,
            transcendentals=0,
        ),
        name="invert",
    )(*operands)


def sum_kernel(count, *refs):
    out = refs[-1]
    total = refs[0][...]
    for part in refs[1:count]:
        total = total + part[...].astype(jnp.float32)
    out[0] = total.astype(out.dtype)


def add(parts, earlier):
    whole = pl.BlockSpec(memory_space=pltpu.VMEM)
    return pl.pallas_call(
        functools.partial(sum_kernel, len(parts)),
        in_specs=[whole] * len(parts) + [pl.BlockSpec(memory_space=pl.ANY)] * len(earlier),
        out_specs=whole,
        out_shape=jax.ShapeDtypeStruct((1, *parts[0].shape), jnp.bfloat16),
        compiler_params=pltpu.CompilerParams(vmem_limit_bytes=S_VMEM),
        name="add",
    )(*parts, *earlier)


def stack_kernel(count, *refs):
    out, place = refs[-1], 0
    for piece in refs[:count]:
        out[pl.ds(place, piece.shape[0])] = piece[...]
        place += piece.shape[0]


def stack(pieces, earlier):
    whole = pl.BlockSpec(memory_space=pltpu.VMEM)
    total = sum(piece.shape[0] for piece in pieces)
    return pl.pallas_call(
        functools.partial(stack_kernel, len(pieces)),
        in_specs=[whole] * len(pieces) + [pl.BlockSpec(memory_space=pl.ANY)] * len(earlier),
        out_specs=whole,
        out_shape=jax.ShapeDtypeStruct((total, *pieces[0].shape[1:]), pieces[0].dtype),
        compiler_params=pltpu.CompilerParams(vmem_limit_bytes=S_VMEM),
        name="stack",
    )(*pieces, *earlier)


def swap(array, axis, mask):
    return lax.ppermute(array, axis, [(i, i ^ mask) for i in range(lax.axis_size(axis))])


def on_device(traces, reflection, onset):
    local_times, focal_count, _ = traces.shape
    freq_devices, mat_devices = lax.axis_size("freq"), lax.axis_size("mat")
    per_device = reflection.shape[0]
    table = tables(per_device, freq_devices, local_times)
    focal = focal_count // CHUNKS

    steps = [1 << bit for bit in reversed(range(1, mat_devices.bit_length() - 1))]

    parts = [forward(table, traces, i * focal, focal, per_device, freq_devices) for i in range(CHUNKS)]
    spectra = []
    for i, part in enumerate(parts):
        arrived = [swap(part[mask], "freq", mask) for mask in range(1, freq_devices)]
        spectra.append(add([part[0], *arrived], [later[0] for later in parts[i + 1 :]]))
    held, masks, tied = [], [0], []
    for block in spectra:
        for step in steps[:-1]:
            block = stack([block, swap(block, "mat", step)], tied or [spectra[-1]])
        if not tied:
            tied = [spread(table), load(reflection, [block])]
        held.append((block, swap(block, "mat", steps[-1])))
    for step in steps[:-1]:
        masks = masks + [mask ^ step for mask in masks]
    masks = [masks, [mask ^ steps[-1] for mask in masks]]
    masks += [[mask ^ 1 for mask in some] for some in masks]

    inverse_spread, loaded = tied
    responses = []
    for i, (block, other) in enumerate(held):
        if responses:
            other = stack([other], [responses[-1][0]])
        pieces = [block, other, swap(block, "mat", 1), swap(other, "mat", 1)]
        response = respond(loaded, pieces, masks, [later for later, _ in held[i + 1 :]])
        responses.append([response] + [swap(response, "freq", mask) for mask in range(1, freq_devices)])
    windowed = None
    for i, pieces in enumerate(responses):
        windowed = invert(inverse_spread, onset, pieces, windowed, i * focal, traces.shape)
    return windowed


def solution(mesh):
    placed = (P("freq", None, "mat"), P("freq", None, "mat", None), P(None, "mat"))
    return jax.shard_map(
        on_device, mesh=mesh, in_specs=placed, out_specs=P("freq", None, "mat"), check_vma=False
    )
```

```python
import functools
import math

import jax
import jax.numpy as jnp
from jax import lax
from jax.experimental import pallas as pl
from jax.experimental.pallas import tpu as pltpu
from jax.sharding import PartitionSpec as P

ROWS = 16
CHUNKS = 2
F_TIMES = 256
F_SLOTS = 3
I_TIMES = 128
I_SLOTS = 3
I_CUTS = 4
MIB = 1024 * 1024
F_VMEM = 40 * MIB
R_VMEM = 12 * MIB
I_VMEM = 20 * MIB
S_VMEM = 16 * MIB
L_VMEM = 32 * MIB


def phases(bands, times, samples):
    return (bands * times % samples).astype(jnp.float32) * (2.0 * math.pi / samples)


def tables(per_device, freq_devices, local_times):
    me = lax.axis_index("freq")
    samples = local_times * freq_devices
    owners = me ^ jnp.arange(freq_devices, dtype=jnp.int32)
    bands = samples // 16 + (owners[:, None] * per_device + jnp.arange(per_device, dtype=jnp.int32)).reshape(-1)
    times = me * local_times + jnp.arange(local_times, dtype=jnp.int32)
    angles = phases(bands[:, None], times[None, :], samples)
    parts = jnp.stack([jnp.cos(angles), -jnp.sin(angles)], axis=1).reshape(-1, local_times)
    factors = (1.0 / math.sqrt(samples), 1.0 / math.sqrt(per_device * freq_devices))
    return jnp.stack([parts * factor for factor in factors]).astype(jnp.bfloat16)


def repeats(count):
    lane = lax.broadcasted_iota(jnp.int32, (count, count * ROWS), 1)
    row = lax.broadcasted_iota(jnp.int32, (count, count * ROWS), 0)
    return jnp.where(lane // ROWS == row, 1.0, 0.0).astype(jnp.bfloat16)


def spread_rows(store, wide):
    lane = lax.broadcasted_iota(jnp.int32, (ROWS, wide.shape[1]), 1)
    row = lax.broadcasted_iota(jnp.int32, (ROWS, wide.shape[1]), 0)
    own = lane % ROWS == row
    for i in range(wide.shape[0]):
        store(i, jnp.where(own, wide[i : i + 1], 0.0).astype(jnp.bfloat16))


def forward_kernel(first, focal, table_ref, traces_ref, *refs):
    *outs, spread, total, slots, sems = refs
    depth, times, rows, width = slots.shape
    steps = spread.shape[0]
    count = steps * (focal // rows)

    def fetch(i):
        slot = lax.rem(i, depth)
        source = traces_ref.at[
            pl.ds(lax.rem(i, steps) * times, times), pl.ds(first + i // steps * rows, rows), :
        ]
        return pltpu.make_async_copy(source, slots.at[slot], sems.at[slot])

    for i in range(min(depth - 1, count)):
        fetch(jnp.int32(i)).start()

    for step in range(steps):

        def store(i, block, step=step):
            spread[step, pl.ds(i * rows, rows), :] = block

        some = table_ref[0, :, pl.ds(step * times, times)]
        spread_rows(store, jnp.dot(some, repeats(times), preferred_element_type=jnp.float32))

    @pl.loop(0, count)
    def _(i):
        step = lax.rem(i, steps)

        @pl.when(i + depth - 1 < count)
        def _():
            fetch(i + depth - 1).start()

        fetch(i).wait()
        block = slots[lax.rem(i, depth)].reshape(times * rows, width)
        part = jnp.dot(spread[step], block, preferred_element_type=jnp.float32)

        @pl.when(step == 0)
        def _():
            total[...] = part

        @pl.when(step > 0)
        def _():
            total[...] += part

        @pl.when(step == steps - 1)
        def _():
            share = total.shape[0] // len(outs)
            place = pl.ds(pl.multiple_of(i // steps * rows, rows), rows)
            for j, out in enumerate(outs):
                value = total[pl.ds(j * share, share), :].reshape(*out.shape[:2], rows, width)
                out[:, :, place, :] = value.astype(out.dtype)


def forward(table, traces, first, focal, per_device, freq_devices):
    local_times, _, width = traces.shape
    times = min(F_TIMES, local_times)
    steps = local_times // times
    count = 2 * per_device * freq_devices
    shape = (per_device, 2, focal, width)
    whole = pl.BlockSpec(memory_space=pltpu.VMEM)
    return pl.pallas_call(
        functools.partial(forward_kernel, first, focal),
        in_specs=[whole, pl.BlockSpec(memory_space=pl.ANY)],
        out_specs=[whole] * freq_devices,
        out_shape=[jax.ShapeDtypeStruct(shape, jnp.float32 if i == 0 else jnp.bfloat16) for i in range(freq_devices)],
        scratch_shapes=[
            pltpu.VMEM((steps, count * ROWS, times * ROWS), jnp.bfloat16),
            pltpu.VMEM((count * ROWS, width), jnp.float32),
            pltpu.VMEM((F_SLOTS, times, ROWS, width), jnp.bfloat16),
            pltpu.SemaphoreType.DMA((F_SLOTS,)),
        ],
        compiler_params=pltpu.CompilerParams(vmem_limit_bytes=F_VMEM),
        cost_estimate=pl.CostEstimate(
            flops=2 * count * ROWS * local_times * focal * width,
            bytes_accessed=2 * local_times * focal * width,
            transcendentals=0,
        ),
        name="forward",
    )(table, traces)


def load_kernel(reflection_ref, *refs):
    out, sems = refs[-2:]

    def fetch(i):
        return pltpu.make_async_copy(reflection_ref.at[i], out.at[i], sems.at[i])

    for i in range(out.shape[0]):
        fetch(i).start()
    for i in range(out.shape[0]):
        fetch(i).wait()


def load(reflection, earlier):
    return pl.pallas_call(
        load_kernel,
        in_specs=[pl.BlockSpec(memory_space=pl.ANY)] * (1 + len(earlier)),
        out_specs=pl.BlockSpec(memory_space=pltpu.VMEM),
        out_shape=jax.ShapeDtypeStruct(reflection.shape, reflection.dtype),
        scratch_shapes=[pltpu.SemaphoreType.DMA((reflection.shape[0],))],
        compiler_params=pltpu.CompilerParams(vmem_limit_bytes=L_VMEM),
        name="load",
    )(reflection, *earlier)


def response_kernel(masks, reflection_ref, *refs):
    out, spectra = refs[-2:]
    bands, _, rows, sources = reflection_ref.shape
    _, _, _, focal, width = refs[0].shape
    me = lax.axis_index("mat")
    for pieces, origins in zip(refs, masks):
        for i, mask in enumerate(origins):
            start = pl.multiple_of((me ^ mask) * width, width)
            spectra[:, :, pl.ds(start, width)] = pieces[i].reshape(bands, 2 * focal, width)
    for band in range(bands):
        product = lax.dot_general(
            reflection_ref[band].reshape(2 * rows, sources),
            spectra[band],
            (((1,), (1,)), ((), ())),
            preferred_element_type=jnp.float32,
        ).T
        out[band, 0] = (product[:focal, :rows] - product[focal:, rows:]).astype(out.dtype)
        out[band, 1] = (product[focal:, :rows] + product[:focal, rows:]).astype(out.dtype)


def respond(reflection, pieces, masks, earlier):
    per_device, _, rows, sources = reflection.shape
    focal, width = pieces[0].shape[3:]
    whole = pl.BlockSpec(memory_space=pltpu.VMEM)
    return pl.pallas_call(
        functools.partial(response_kernel, masks),
        in_specs=[whole] * (1 + len(pieces)) + [pl.BlockSpec(memory_space=pl.ANY)] * len(earlier),
        out_specs=whole,
        out_shape=jax.ShapeDtypeStruct((per_device, 2, focal, rows), jnp.bfloat16),
        scratch_shapes=[pltpu.VMEM((per_device, 2 * focal, sources), jnp.bfloat16)],
        compiler_params=pltpu.CompilerParams(vmem_limit_bytes=R_VMEM),
        cost_estimate=pl.CostEstimate(flops=0, bytes_accessed=1024, transcendentals=0),
        name="respond",
    )(reflection, *pieces, *earlier)


def half_kernel(masks, last, reflection_ref, own_ref, other_ref, *refs):
    out, spectra = refs[-2:]
    bands, _, rows, _ = reflection_ref.shape
    _, _, _, focal, width = own_ref.shape
    me = lax.axis_index("mat")
    for i in range(len(masks)):
        for core, pieces in enumerate((own_ref, other_ref)):
            start = pl.multiple_of((me % 2 ^ core) * width, width)
            spectra[i, :, :, pl.ds(start, width)] = pieces[i].reshape(bands, 2 * focal, width)
    for band in range(bands):
        total = refs[0][band] if last else None
        for i, mask in enumerate(masks):
            start = pl.multiple_of((me ^ mask) // 2 * 2 * width, 2 * width)
            part = lax.dot_general(
                reflection_ref[band, :, :, pl.ds(start, 2 * width)].reshape(2 * rows, 2 * width),
                spectra[i, band],
                (((1,), (1,)), ((), ())),
                preferred_element_type=jnp.float32,
            )
            total = part if total is None else total + part
        if last:
            product = total.T
            out[band, 0] = (product[:focal, :rows] - product[focal:, rows:]).astype(out.dtype)
            out[band, 1] = (product[focal:, :rows] + product[:focal, rows:]).astype(out.dtype)
        else:
            out[band] = total


def respond_half(reflection, own, other, masks, before, earlier):
    per_device, _, rows, sources = reflection.shape
    focal, width = own.shape[3:]
    whole = pl.BlockSpec(memory_space=pltpu.VMEM)
    if before is None:
        shape = jax.ShapeDtypeStruct((per_device, 2 * rows, 2 * focal), jnp.float32)
        given = []
    else:
        shape = jax.ShapeDtypeStruct((per_device, 2, focal, rows), jnp.bfloat16)
        given = [before]
    return pl.pallas_call(
        functools.partial(half_kernel, masks, before is not None),
        in_specs=[whole] * (3 + len(given)) + [pl.BlockSpec(memory_space=pl.ANY)] * len(earlier),
        out_specs=whole,
        out_shape=shape,
        scratch_shapes=[pltpu.VMEM((len(masks), per_device, 2 * focal, 2 * width), jnp.bfloat16)],
        compiler_params=pltpu.CompilerParams(vmem_limit_bytes=R_VMEM),
        cost_estimate=pl.CostEstimate(flops=0, bytes_accessed=1024, transcendentals=0),
        name="respond_half",
    )(reflection, own, other, *given, *earlier)


def spread_kernel(table_ref, out):
    def store(i, block):
        out[pl.ds(i * ROWS, ROWS), :] = block

    table = table_ref[1]
    wide = lax.dot_general(
        table, repeats(table.shape[0]), (((0,), (0,)), ((), ())), preferred_element_type=jnp.float32
    )
    spread_rows(store, wide)


def spread(table):
    _, count, times = table.shape
    whole = pl.BlockSpec(memory_space=pltpu.VMEM)
    return pl.pallas_call(
        spread_kernel,
        in_specs=[whole],
        out_specs=whole,
        out_shape=jax.ShapeDtypeStruct((times * ROWS, count * ROWS), jnp.bfloat16),
        compiler_params=pltpu.CompilerParams(vmem_limit_bytes=S_VMEM),
        cost_estimate=pl.CostEstimate(flops=0, bytes_accessed=2 * times * ROWS * count * ROWS, transcendentals=0),
        name="spread",
    )(table)


def inverse_kernel(first, has_before, spread, onset_ref, *refs):
    pieces, (out, weights, slots, sems) = refs[: -4 - has_before], refs[-4:]
    depth, times, rows, width = slots.shape
    cuts = sems.shape[1]
    some = times // cuts
    focal = pieces[0].shape[2]
    local_times = out.shape[0]
    steps = local_times // times
    count = steps * (focal // rows)
    share = weights.shape[0] // len(pieces)
    begin = lax.axis_index("freq") * local_times

    def send(i, cut):
        slot = lax.rem(i, depth)
        start = lax.rem(i, steps) * times + cut * some
        target = out.at[pl.ds(start, some), pl.ds(first + i // steps * rows, rows), :]
        return pltpu.make_async_copy(slots.at[slot, pl.ds(cut * some, some)], target, sems.at[slot, cut])

    @pl.loop(0, count)
    def _(i):
        step = lax.rem(i, steps)
        slot = lax.rem(i, depth)
        place = pl.ds(pl.multiple_of(i // steps * rows, rows), rows)

        @pl.when(i >= depth)
        def _():
            for cut in range(cuts):
                send(i - depth, cut).wait()

        @pl.when(step == 0)
        def _():
            for j, piece in enumerate(pieces):
                weights[pl.ds(j * share, share), :] = piece[:, :, place, :].reshape(share, width)

        onset = onset_ref[pl.ds(pl.multiple_of(first + i // steps * rows, rows), rows), :]
        for cut in range(cuts):
            start = step * times + cut * some
            lines = pl.ds(pl.multiple_of(start * rows, some * rows), some * rows)
            signal = jnp.dot(spread[lines, :], weights[...], preferred_element_type=jnp.float32)
            signal = signal.reshape(some, rows, width)
            moment = begin + start + lax.broadcasted_iota(jnp.int32, (some, 1, 1), 0)
            windowed = jnp.where(moment < onset[None], signal, 0.0).astype(out.dtype)
            slots[slot, pl.ds(cut * some, some)] = windowed
            send(i, cut).start()

    for i in range(max(0, count - depth), count):
        for cut in range(cuts):
            send(jnp.int32(i), cut).wait()


def invert(table, onset, pieces, before, first, shape):
    local_times, _, width = shape
    focal = pieces[0].shape[2]
    times = min(I_TIMES, local_times)
    has_before = before is not None
    operands = [table, onset, *pieces] + ([before] if has_before else [])
    whole = pl.BlockSpec(memory_space=pltpu.VMEM)
    anywhere = pl.BlockSpec(memory_space=pl.ANY)
    return pl.pallas_call(
        functools.partial(inverse_kernel, first, has_before),
        in_specs=[whole] * (2 + len(pieces)) + [anywhere] * has_before,
        out_specs=anywhere,
        out_shape=jax.ShapeDtypeStruct(shape, jnp.bfloat16),
        scratch_shapes=[
            pltpu.VMEM((table.shape[1], width), jnp.bfloat16),
            pltpu.VMEM((I_SLOTS, times, ROWS, width), jnp.bfloat16),
            pltpu.SemaphoreType.DMA((I_SLOTS, I_CUTS)),
        ],
        input_output_aliases={len(operands) - 1: 0} if has_before else {},
        compiler_params=pltpu.CompilerParams(vmem_limit_bytes=I_VMEM),
        cost_estimate=pl.CostEstimate(
            flops=2 * table.shape[1] * local_times * focal * width,
            bytes_accessed=2 * local_times * focal * width,
            transcendentals=0,
        ),
        name="invert",
    )(*operands)


def sum_kernel(count, *refs):
    out = refs[-1]
    total = refs[0][...]
    for part in refs[1:count]:
        total = total + part[...].astype(jnp.float32)
    out[0] = total.astype(out.dtype)


def add(parts, earlier):
    whole = pl.BlockSpec(memory_space=pltpu.VMEM)
    return pl.pallas_call(
        functools.partial(sum_kernel, len(parts)),
        in_specs=[whole] * len(parts) + [pl.BlockSpec(memory_space=pl.ANY)] * len(earlier),
        out_specs=whole,
        out_shape=jax.ShapeDtypeStruct((1, *parts[0].shape), jnp.bfloat16),
        compiler_params=pltpu.CompilerParams(vmem_limit_bytes=S_VMEM),
        name="add",
    )(*parts, *earlier)


def stack_kernel(count, *refs):
    out, place = refs[-1], 0
    for piece in refs[:count]:
        out[pl.ds(place, piece.shape[0])] = piece[...]
        place += piece.shape[0]


def stack(pieces, earlier):
    whole = pl.BlockSpec(memory_space=pltpu.VMEM)
    total = sum(piece.shape[0] for piece in pieces)
    return pl.pallas_call(
        functools.partial(stack_kernel, len(pieces)),
        in_specs=[whole] * len(pieces) + [pl.BlockSpec(memory_space=pl.ANY)] * len(earlier),
        out_specs=whole,
        out_shape=jax.ShapeDtypeStruct((total, *pieces[0].shape[1:]), pieces[0].dtype),
        compiler_params=pltpu.CompilerParams(vmem_limit_bytes=S_VMEM),
        name="stack",
    )(*pieces, *earlier)


def swap(array, axis, mask):
    return lax.ppermute(array, axis, [(i, i ^ mask) for i in range(lax.axis_size(axis))])


def on_device(traces, reflection, onset):
    local_times, focal_count, _ = traces.shape
    freq_devices, mat_devices = lax.axis_size("freq"), lax.axis_size("mat")
    per_device = reflection.shape[0]
    table = tables(per_device, freq_devices, local_times)
    focal = focal_count // CHUNKS

    steps = [1 << bit for bit in reversed(range(1, mat_devices.bit_length() - 1))]

    parts = [forward(table, traces, i * focal, focal, per_device, freq_devices) for i in range(CHUNKS)]
    spectra = []
    inverse_spread = spread(table)
    for i, part in enumerate(parts):
        arrived = [swap(part[mask], "freq", mask) for mask in range(1, freq_devices)]
        spectra.append(add([part[0], *arrived], [later[0] for later in parts[i + 1 :]] or [inverse_spread]))
    held, masks, tied = [], [0], []
    for block in spectra:
        for step in steps[:-1]:
            block = stack([block, swap(block, "mat", step)], tied or [spectra[-1]])
        if not tied:
            tied = [load(reflection, [block])]
        held.append((block, swap(block, "mat", steps[-1])))
    for step in steps[:-1]:
        masks = masks + [mask ^ step for mask in masks]
    masks = [masks, [mask ^ steps[-1] for mask in masks]]
    masks += [[mask ^ 1 for mask in some] for some in masks]

    loaded = tied[0]
    responses = []
    for i, (block, other) in enumerate(held):
        beside = swap(block, "mat", 1)
        if responses:
            half = respond_half(loaded, block, beside, masks[0], None, [responses[-1][0]])
            other = stack([other], [half])
            response = respond_half(loaded, other, swap(other, "mat", 1), masks[1], half, [])
        else:
            pieces = [block, other, beside, swap(other, "mat", 1)]
            response = respond(loaded, pieces, masks, [later for later, _ in held[i + 1 :]])
        responses.append([response] + [swap(response, "freq", mask) for mask in range(1, freq_devices)])
    windowed = None
    for i, pieces in enumerate(responses):
        windowed = invert(inverse_spread, onset, pieces, windowed, i * focal, traces.shape)
    return windowed


def solution(mesh):
    placed = (P("freq", None, "mat"), P("freq", None, "mat", None), P(None, "mat"))
    return jax.shard_map(
        on_device, mesh=mesh, in_specs=placed, out_specs=P("freq", None, "mat"), check_vma=False
    )
```

```python
import functools
import math

import jax
import jax.numpy as jnp
from jax import lax
from jax.experimental import pallas as pl
from jax.experimental.pallas import tpu as pltpu
from jax.sharding import PartitionSpec as P

ROWS = 16
CHUNKS = 2
F_TIMES = 256
F_SLOTS = 3
I_TIMES = 128
I_SLOTS = 3
I_CUTS = 4
MIB = 1024 * 1024
F_VMEM = 40 * MIB
R_VMEM = 12 * MIB
I_VMEM = 20 * MIB
S_VMEM = 16 * MIB
L_VMEM = 32 * MIB


def phases(bands, times, samples):
    return (bands * times % samples).astype(jnp.float32) * (2.0 * math.pi / samples)


def tables(per_device, freq_devices, local_times):
    me = lax.axis_index("freq")
    samples = local_times * freq_devices
    owners = me ^ jnp.arange(freq_devices, dtype=jnp.int32)
    bands = samples // 16 + (owners[:, None] * per_device + jnp.arange(per_device, dtype=jnp.int32)).reshape(-1)
    times = me * local_times + jnp.arange(local_times, dtype=jnp.int32)
    angles = phases(bands[:, None], times[None, :], samples)
    parts = jnp.stack([jnp.cos(angles), -jnp.sin(angles)], axis=1).reshape(-1, local_times)
    factors = (1.0 / math.sqrt(samples), 1.0 / math.sqrt(per_device * freq_devices))
    return jnp.stack([parts * factor for factor in factors]).astype(jnp.bfloat16)


def repeats(count):
    lane = lax.broadcasted_iota(jnp.int32, (count, count * ROWS), 1)
    row = lax.broadcasted_iota(jnp.int32, (count, count * ROWS), 0)
    return jnp.where(lane // ROWS == row, 1.0, 0.0).astype(jnp.bfloat16)


def spread_rows(store, wide):
    lane = lax.broadcasted_iota(jnp.int32, (ROWS, wide.shape[1]), 1)
    row = lax.broadcasted_iota(jnp.int32, (ROWS, wide.shape[1]), 0)
    own = lane % ROWS == row
    for i in range(wide.shape[0]):
        store(i, jnp.where(own, wide[i : i + 1], 0.0).astype(jnp.bfloat16))


def forward_kernel(first, focal, table_ref, traces_ref, *refs):
    *outs, spread, total, slots, sems = refs
    depth, times, rows, width = slots.shape
    steps = spread.shape[0]
    count = steps * (focal // rows)

    def fetch(i):
        slot = lax.rem(i, depth)
        source = traces_ref.at[
            pl.ds(lax.rem(i, steps) * times, times), pl.ds(first + i // steps * rows, rows), :
        ]
        return pltpu.make_async_copy(source, slots.at[slot], sems.at[slot])

    for i in range(min(depth - 1, count)):
        fetch(jnp.int32(i)).start()

    for step in range(steps):

        def store(i, block, step=step):
            spread[step, pl.ds(i * rows, rows), :] = block

        some = table_ref[0, :, pl.ds(step * times, times)]
        spread_rows(store, jnp.dot(some, repeats(times), preferred_element_type=jnp.float32))

    @pl.loop(0, count)
    def _(i):
        step = lax.rem(i, steps)

        @pl.when(i + depth - 1 < count)
        def _():
            fetch(i + depth - 1).start()

        fetch(i).wait()
        block = slots[lax.rem(i, depth)].reshape(times * rows, width)
        part = jnp.dot(spread[step], block, preferred_element_type=jnp.float32)

        @pl.when(step == 0)
        def _():
            total[...] = part

        @pl.when(step > 0)
        def _():
            total[...] += part

        @pl.when(step == steps - 1)
        def _():
            share = total.shape[0] // len(outs)
            place = pl.ds(pl.multiple_of(i // steps * rows, rows), rows)
            for j, out in enumerate(outs):
                value = total[pl.ds(j * share, share), :].reshape(*out.shape[:2], rows, width)
                out[:, :, place, :] = value.astype(out.dtype)


def forward(table, traces, first, focal, per_device, freq_devices):
    local_times, _, width = traces.shape
    times = min(F_TIMES, local_times)
    steps = local_times // times
    count = 2 * per_device * freq_devices
    shape = (per_device, 2, focal, width)
    whole = pl.BlockSpec(memory_space=pltpu.VMEM)
    return pl.pallas_call(
        functools.partial(forward_kernel, first, focal),
        in_specs=[whole, pl.BlockSpec(memory_space=pl.ANY)],
        out_specs=[whole] * freq_devices,
        out_shape=[jax.ShapeDtypeStruct(shape, jnp.float32 if i == 0 else jnp.bfloat16) for i in range(freq_devices)],
        scratch_shapes=[
            pltpu.VMEM((steps, count * ROWS, times * ROWS), jnp.bfloat16),
            pltpu.VMEM((count * ROWS, width), jnp.float32),
            pltpu.VMEM((F_SLOTS, times, ROWS, width), jnp.bfloat16),
            pltpu.SemaphoreType.DMA((F_SLOTS,)),
        ],
        compiler_params=pltpu.CompilerParams(vmem_limit_bytes=F_VMEM),
        cost_estimate=pl.CostEstimate(
            flops=2 * count * ROWS * local_times * focal * width,
            bytes_accessed=2 * local_times * focal * width,
            transcendentals=0,
        ),
        name="forward",
    )(table, traces)


def load_kernel(first, reflection_ref, *refs):
    out, sems = refs[-2:]
    bands, parts = out.shape[:2]

    def fetch(band, part):
        return pltpu.make_async_copy(reflection_ref.at[first + band, part], out.at[band, part], sems.at[band, part])

    for band in range(bands):
        for part in range(parts):
            fetch(band, part).start()
    for band in range(bands):
        for part in range(parts):
            fetch(band, part).wait()


def load(reflection, first, bands, earlier):
    return pl.pallas_call(
        functools.partial(load_kernel, first),
        in_specs=[pl.BlockSpec(memory_space=pl.ANY)] * (1 + len(earlier)),
        out_specs=pl.BlockSpec(memory_space=pltpu.VMEM),
        out_shape=jax.ShapeDtypeStruct((bands, *reflection.shape[1:]), reflection.dtype),
        scratch_shapes=[pltpu.SemaphoreType.DMA((bands, reflection.shape[1]))],
        compiler_params=pltpu.CompilerParams(vmem_limit_bytes=L_VMEM),
        name="load",
    )(reflection, *earlier)


def response_kernel(masks, loads, *refs):
    kept, refs = refs[:loads], refs[loads:]
    out, spectra = refs[-2:]
    share, _, rows, sources = kept[0].shape
    _, bands, _, focal, width = refs[0].shape
    me = lax.axis_index("mat")
    for pieces, origins in zip(refs, masks):
        for i, mask in enumerate(origins):
            start = pl.multiple_of((me ^ mask) * width, width)
            spectra[:, :, pl.ds(start, width)] = pieces[i].reshape(bands, 2 * focal, width)
    for band in range(bands):
        product = lax.dot_general(
            kept[band // share][band % share].reshape(2 * rows, sources),
            spectra[band],
            (((1,), (1,)), ((), ())),
            preferred_element_type=jnp.float32,
        ).T
        out[band, 0] = (product[:focal, :rows] - product[focal:, rows:]).astype(out.dtype)
        out[band, 1] = (product[focal:, :rows] + product[:focal, rows:]).astype(out.dtype)


def respond(kept, pieces, masks, earlier):
    _, _, rows, sources = kept[0].shape
    _, per_device, _, focal, width = pieces[0].shape
    whole = pl.BlockSpec(memory_space=pltpu.VMEM)
    return pl.pallas_call(
        functools.partial(response_kernel, masks, len(kept)),
        in_specs=[whole] * (len(kept) + len(pieces)) + [pl.BlockSpec(memory_space=pl.ANY)] * len(earlier),
        out_specs=whole,
        out_shape=jax.ShapeDtypeStruct((per_device, 2, focal, rows), jnp.bfloat16),
        scratch_shapes=[pltpu.VMEM((per_device, 2 * focal, sources), jnp.bfloat16)],
        compiler_params=pltpu.CompilerParams(vmem_limit_bytes=R_VMEM),
        cost_estimate=pl.CostEstimate(flops=0, bytes_accessed=1024, transcendentals=0),
        name="respond",
    )(*kept, *pieces, *earlier)


def half_kernel(masks, last, loads, own_ref, other_ref, *refs):
    kept, (out, spectra) = refs[last : last + loads], refs[-2:]
    share, _, rows, _ = kept[0].shape
    _, bands, _, focal, width = own_ref.shape
    me = lax.axis_index("mat")
    for i in range(len(masks)):
        for core, pieces in enumerate((own_ref, other_ref)):
            start = pl.multiple_of((me % 2 ^ core) * width, width)
            spectra[i, :, :, pl.ds(start, width)] = pieces[i].reshape(bands, 2 * focal, width)
    for band in range(bands):
        total = refs[0][band] if last else None
        for i, mask in enumerate(masks):
            start = pl.multiple_of((me ^ mask) // 2 * 2 * width, 2 * width)
            part = lax.dot_general(
                kept[band // share][band % share, :, :, pl.ds(start, 2 * width)].reshape(2 * rows, 2 * width),
                spectra[i, band],
                (((1,), (1,)), ((), ())),
                preferred_element_type=jnp.float32,
            )
            total = part if total is None else total + part
        if last:
            product = total.T
            out[band, 0] = (product[:focal, :rows] - product[focal:, rows:]).astype(out.dtype)
            out[band, 1] = (product[focal:, :rows] + product[:focal, rows:]).astype(out.dtype)
        else:
            out[band] = total


def respond_half(kept, own, other, masks, before, earlier):
    _, _, rows, _ = kept[0].shape
    _, per_device, _, focal, width = own.shape
    whole = pl.BlockSpec(memory_space=pltpu.VMEM)
    if before is None:
        shape = jax.ShapeDtypeStruct((per_device, 2 * rows, 2 * focal), jnp.float32)
        given = []
    else:
        shape = jax.ShapeDtypeStruct((per_device, 2, focal, rows), jnp.bfloat16)
        given = [before]
    return pl.pallas_call(
        functools.partial(half_kernel, masks, before is not None, len(kept)),
        in_specs=[whole] * (2 + len(given) + len(kept)) + [pl.BlockSpec(memory_space=pl.ANY)] * len(earlier),
        out_specs=whole,
        out_shape=shape,
        scratch_shapes=[pltpu.VMEM((len(masks), per_device, 2 * focal, 2 * width), jnp.bfloat16)],
        compiler_params=pltpu.CompilerParams(vmem_limit_bytes=R_VMEM),
        cost_estimate=pl.CostEstimate(flops=0, bytes_accessed=1024, transcendentals=0),
        name="respond_half",
    )(own, other, *given, *kept, *earlier)


def spread_kernel(table_ref, out):
    def store(i, block):
        out[pl.ds(i * ROWS, ROWS), :] = block

    table = table_ref[1]
    wide = lax.dot_general(
        table, repeats(table.shape[0]), (((0,), (0,)), ((), ())), preferred_element_type=jnp.float32
    )
    spread_rows(store, wide)


def spread(table):
    _, count, times = table.shape
    whole = pl.BlockSpec(memory_space=pltpu.VMEM)
    return pl.pallas_call(
        spread_kernel,
        in_specs=[whole],
        out_specs=whole,
        out_shape=jax.ShapeDtypeStruct((times * ROWS, count * ROWS), jnp.bfloat16),
        compiler_params=pltpu.CompilerParams(vmem_limit_bytes=S_VMEM),
        cost_estimate=pl.CostEstimate(flops=0, bytes_accessed=2 * times * ROWS * count * ROWS, transcendentals=0),
        name="spread",
    )(table)


def inverse_kernel(first, has_before, spread, onset_ref, *refs):
    pieces, (out, weights, slots, sems) = refs[: -4 - has_before], refs[-4:]
    depth, times, rows, width = slots.shape
    cuts = sems.shape[1]
    some = times // cuts
    focal = pieces[0].shape[2]
    local_times = out.shape[0]
    steps = local_times // times
    count = steps * (focal // rows)
    share = weights.shape[0] // len(pieces)
    begin = lax.axis_index("freq") * local_times

    def send(i, cut):
        slot = lax.rem(i, depth)
        start = lax.rem(i, steps) * times + cut * some
        target = out.at[pl.ds(start, some), pl.ds(first + i // steps * rows, rows), :]
        return pltpu.make_async_copy(slots.at[slot, pl.ds(cut * some, some)], target, sems.at[slot, cut])

    @pl.loop(0, count)
    def _(i):
        step = lax.rem(i, steps)
        slot = lax.rem(i, depth)
        place = pl.ds(pl.multiple_of(i // steps * rows, rows), rows)

        @pl.when(i >= depth)
        def _():
            for cut in range(cuts):
                send(i - depth, cut).wait()

        @pl.when(step == 0)
        def _():
            for j, piece in enumerate(pieces):
                weights[pl.ds(j * share, share), :] = piece[:, :, place, :].reshape(share, width)

        onset = onset_ref[pl.ds(pl.multiple_of(first + i // steps * rows, rows), rows), :]
        for cut in range(cuts):
            start = step * times + cut * some
            lines = pl.ds(pl.multiple_of(start * rows, some * rows), some * rows)
            signal = jnp.dot(spread[lines, :], weights[...], preferred_element_type=jnp.float32)
            signal = signal.reshape(some, rows, width)
            moment = begin + start + lax.broadcasted_iota(jnp.int32, (some, 1, 1), 0)
            windowed = jnp.where(moment < onset[None], signal, 0.0).astype(out.dtype)
            slots[slot, pl.ds(cut * some, some)] = windowed
            send(i, cut).start()

    for i in range(max(0, count - depth), count):
        for cut in range(cuts):
            send(jnp.int32(i), cut).wait()


def invert(table, onset, pieces, before, first, shape):
    local_times, _, width = shape
    focal = pieces[0].shape[2]
    times = min(I_TIMES, local_times)
    has_before = before is not None
    operands = [table, onset, *pieces] + ([before] if has_before else [])
    whole = pl.BlockSpec(memory_space=pltpu.VMEM)
    anywhere = pl.BlockSpec(memory_space=pl.ANY)
    return pl.pallas_call(
        functools.partial(inverse_kernel, first, has_before),
        in_specs=[whole] * (2 + len(pieces)) + [anywhere] * has_before,
        out_specs=anywhere,
        out_shape=jax.ShapeDtypeStruct(shape, jnp.bfloat16),
        scratch_shapes=[
            pltpu.VMEM((table.shape[1], width), jnp.bfloat16),
            pltpu.VMEM((I_SLOTS, times, ROWS, width), jnp.bfloat16),
            pltpu.SemaphoreType.DMA((I_SLOTS, I_CUTS)),
        ],
        input_output_aliases={len(operands) - 1: 0} if has_before else {},
        compiler_params=pltpu.CompilerParams(vmem_limit_bytes=I_VMEM),
        cost_estimate=pl.CostEstimate(
            flops=2 * table.shape[1] * local_times * focal * width,
            bytes_accessed=2 * local_times * focal * width,
            transcendentals=0,
        ),
        name="invert",
    )(*operands)


def sum_kernel(count, *refs):
    out = refs[-1]
    total = refs[0][...]
    for part in refs[1:count]:
        total = total + part[...].astype(jnp.float32)
    out[0] = total.astype(out.dtype)


def add(parts, earlier):
    whole = pl.BlockSpec(memory_space=pltpu.VMEM)
    return pl.pallas_call(
        functools.partial(sum_kernel, len(parts)),
        in_specs=[whole] * len(parts) + [pl.BlockSpec(memory_space=pl.ANY)] * len(earlier),
        out_specs=whole,
        out_shape=jax.ShapeDtypeStruct((1, *parts[0].shape), jnp.bfloat16),
        compiler_params=pltpu.CompilerParams(vmem_limit_bytes=S_VMEM),
        name="add",
    )(*parts, *earlier)


def stack_kernel(count, *refs):
    out, place = refs[-1], 0
    for piece in refs[:count]:
        out[pl.ds(place, piece.shape[0])] = piece[...]
        place += piece.shape[0]


def stack(pieces, earlier):
    whole = pl.BlockSpec(memory_space=pltpu.VMEM)
    total = sum(piece.shape[0] for piece in pieces)
    return pl.pallas_call(
        functools.partial(stack_kernel, len(pieces)),
        in_specs=[whole] * len(pieces) + [pl.BlockSpec(memory_space=pl.ANY)] * len(earlier),
        out_specs=whole,
        out_shape=jax.ShapeDtypeStruct((total, *pieces[0].shape[1:]), pieces[0].dtype),
        compiler_params=pltpu.CompilerParams(vmem_limit_bytes=S_VMEM),
        name="stack",
    )(*pieces, *earlier)


def swap(array, axis, mask):
    return lax.ppermute(array, axis, [(i, i ^ mask) for i in range(lax.axis_size(axis))])


def on_device(traces, reflection, onset):
    local_times, focal_count, _ = traces.shape
    freq_devices, mat_devices = lax.axis_size("freq"), lax.axis_size("mat")
    per_device = reflection.shape[0]
    table = tables(per_device, freq_devices, local_times)
    focal = focal_count // CHUNKS

    steps = [1 << bit for bit in reversed(range(1, mat_devices.bit_length() - 1))]

    parts = [forward(table, traces, i * focal, focal, per_device, freq_devices) for i in range(CHUNKS)]
    spectra = []
    inverse_spread = spread(table)
    some = max(1, per_device // 2)
    kept = []
    for i, part in enumerate(parts):
        arrived = [swap(part[mask], "freq", mask) for mask in range(1, freq_devices)]
        if spectra:
            kept.append(load(reflection, 0, some, [spectra[0]]))
        spectra.append(add([part[0], *arrived], [later[0] for later in parts[i + 1 :]] or [inverse_spread, *kept]))
    held, masks, tied = [], [0], []
    for block in spectra:
        for step in steps[:-1]:
            block = stack([block, swap(block, "mat", step)], tied or [spectra[-1]])
        if not tied:
            tied = [load(reflection, some, per_device - some, [spectra[-1]])]
        held.append((block, swap(block, "mat", steps[-1])))
    for step in steps[:-1]:
        masks = masks + [mask ^ step for mask in masks]
    masks = [masks, [mask ^ steps[-1] for mask in masks]]
    masks += [[mask ^ 1 for mask in some] for some in masks]

    kept += tied
    responses = []
    for i, (block, other) in enumerate(held):
        beside = swap(block, "mat", 1)
        if responses:
            half = respond_half(kept, block, beside, masks[0], None, [responses[-1][0]])
            other = stack([other], [half])
            response = respond_half(kept, other, swap(other, "mat", 1), masks[1], half, [])
        else:
            pieces = [block, other, beside, swap(other, "mat", 1)]
            response = respond(kept, pieces, masks, [later for later, _ in held[i + 1 :]])
        responses.append([response] + [swap(response, "freq", mask) for mask in range(1, freq_devices)])
    windowed = None
    for i, pieces in enumerate(responses):
        windowed = invert(inverse_spread, onset, pieces, windowed, i * focal, traces.shape)
    return windowed


def solution(mesh):
    placed = (P("freq", None, "mat"), P("freq", None, "mat", None), P(None, "mat"))
    return jax.shard_map(
        on_device, mesh=mesh, in_specs=placed, out_specs=P("freq", None, "mat"), check_vma=False
    )
```

```python
import functools
import math

import jax
import jax.numpy as jnp
from jax import lax
from jax.experimental import pallas as pl
from jax.experimental.pallas import tpu as pltpu
from jax.sharding import PartitionSpec as P

ROWS = 16
CHUNKS = 2
F_TIMES = 256
F_SLOTS = 3
I_TIMES = 256
I_SLOTS = 2
I_CUTS = 8
MIB = 1024 * 1024
F_VMEM = 40 * MIB
R_VMEM = 12 * MIB
I_VMEM = 20 * MIB
S_VMEM = 16 * MIB
L_VMEM = 32 * MIB


def phases(bands, times, samples):
    return (bands * times % samples).astype(jnp.float32) * (2.0 * math.pi / samples)


def tables(per_device, freq_devices, local_times):
    me = lax.axis_index("freq")
    samples = local_times * freq_devices
    owners = me ^ jnp.arange(freq_devices, dtype=jnp.int32)
    bands = samples // 16 + (owners[:, None] * per_device + jnp.arange(per_device, dtype=jnp.int32)).reshape(-1)
    times = me * local_times + jnp.arange(local_times, dtype=jnp.int32)
    angles = phases(bands[:, None], times[None, :], samples)
    parts = jnp.stack([jnp.cos(angles), -jnp.sin(angles)], axis=1).reshape(-1, local_times)
    factors = (1.0 / math.sqrt(samples), 1.0 / math.sqrt(per_device * freq_devices))
    return jnp.stack([parts * factor for factor in factors]).astype(jnp.bfloat16)


def repeats(count):
    lane = lax.broadcasted_iota(jnp.int32, (count, count * ROWS), 1)
    row = lax.broadcasted_iota(jnp.int32, (count, count * ROWS), 0)
    return jnp.where(lane // ROWS == row, 1.0, 0.0).astype(jnp.bfloat16)


def spread_rows(store, wide):
    lane = lax.broadcasted_iota(jnp.int32, (ROWS, wide.shape[1]), 1)
    row = lax.broadcasted_iota(jnp.int32, (ROWS, wide.shape[1]), 0)
    own = lane % ROWS == row
    for i in range(wide.shape[0]):
        store(i, jnp.where(own, wide[i : i + 1], 0.0).astype(jnp.bfloat16))


def forward_kernel(first, focal, table_ref, traces_ref, *refs):
    *outs, spread, total, slots, sems = refs
    depth, times, rows, width = slots.shape
    steps = spread.shape[0]
    count = steps * (focal // rows)

    def fetch(i):
        source = traces_ref.at[pl.ds(i % steps * times, times), pl.ds(first + i // steps * rows, rows), :]
        return pltpu.make_async_copy(source, slots.at[i % depth], sems.at[i % depth])

    for i in range(min(depth - 1, count)):
        fetch(i).start()

    for step in range(steps):

        def store(i, block, step=step):
            spread[step, pl.ds(i * rows, rows), :] = block

        some = table_ref[0, :, pl.ds(step * times, times)]
        spread_rows(store, jnp.dot(some, repeats(times), preferred_element_type=jnp.float32))

    for i in range(count):
        if i + depth - 1 < count:
            fetch(i + depth - 1).start()
        fetch(i).wait()
        step = i % steps
        block = slots[i % depth].reshape(times * rows, width)
        part = jnp.dot(spread[step], block, preferred_element_type=jnp.float32)
        if step > 0:
            part = total[...] + part
        if step < steps - 1:
            total[...] = part
            continue
        share = total.shape[0] // len(outs)
        place = pl.ds(i // steps * rows, rows)
        for j, out in enumerate(outs):
            value = part[j * share : (j + 1) * share].reshape(*out.shape[:2], rows, width)
            out[:, :, place, :] = value.astype(out.dtype)


def forward(table, traces, first, focal, per_device, freq_devices):
    local_times, _, width = traces.shape
    times = min(F_TIMES, local_times)
    steps = local_times // times
    count = 2 * per_device * freq_devices
    shape = (per_device, 2, focal, width)
    whole = pl.BlockSpec(memory_space=pltpu.VMEM)
    return pl.pallas_call(
        functools.partial(forward_kernel, first, focal),
        in_specs=[whole, pl.BlockSpec(memory_space=pl.ANY)],
        out_specs=[whole] * freq_devices,
        out_shape=[jax.ShapeDtypeStruct(shape, jnp.float32 if i == 0 else jnp.bfloat16) for i in range(freq_devices)],
        scratch_shapes=[
            pltpu.VMEM((steps, count * ROWS, times * ROWS), jnp.bfloat16),
            pltpu.VMEM((count * ROWS, width), jnp.float32),
            pltpu.VMEM((F_SLOTS, times, ROWS, width), jnp.bfloat16),
            pltpu.SemaphoreType.DMA((F_SLOTS,)),
        ],
        compiler_params=pltpu.CompilerParams(vmem_limit_bytes=F_VMEM),
        cost_estimate=pl.CostEstimate(
            flops=2 * count * ROWS * local_times * focal * width,
            bytes_accessed=2 * local_times * focal * width,
            transcendentals=0,
        ),
        name="forward",
    )(table, traces)


def load_kernel(first, reflection_ref, *refs):
    out, sems = refs[-2:]
    bands, parts = out.shape[:2]

    def fetch(band, part):
        return pltpu.make_async_copy(reflection_ref.at[first + band, part], out.at[band, part], sems.at[band, part])

    for band in range(bands):
        for part in range(parts):
            fetch(band, part).start()
    for band in range(bands):
        for part in range(parts):
            fetch(band, part).wait()


def load(reflection, first, bands, earlier):
    return pl.pallas_call(
        functools.partial(load_kernel, first),
        in_specs=[pl.BlockSpec(memory_space=pl.ANY)] * (1 + len(earlier)),
        out_specs=pl.BlockSpec(memory_space=pltpu.VMEM),
        out_shape=jax.ShapeDtypeStruct((bands, *reflection.shape[1:]), reflection.dtype),
        scratch_shapes=[pltpu.SemaphoreType.DMA((bands, reflection.shape[1]))],
        compiler_params=pltpu.CompilerParams(vmem_limit_bytes=L_VMEM),
        name="load",
    )(reflection, *earlier)


def response_kernel(masks, loads, *refs):
    kept, refs = refs[:loads], refs[loads:]
    out, spectra = refs[-2:]
    share, _, rows, sources = kept[0].shape
    _, bands, _, focal, width = refs[0].shape
    me = lax.axis_index("mat")
    for pieces, origins in zip(refs, masks):
        for i, mask in enumerate(origins):
            start = pl.multiple_of((me ^ mask) * width, width)
            spectra[:, :, pl.ds(start, width)] = pieces[i].reshape(bands, 2 * focal, width)
    for band in range(bands):
        product = lax.dot_general(
            kept[band // share][band % share].reshape(2 * rows, sources),
            spectra[band],
            (((1,), (1,)), ((), ())),
            preferred_element_type=jnp.float32,
        ).T
        out[band, 0] = (product[:focal, :rows] - product[focal:, rows:]).astype(out.dtype)
        out[band, 1] = (product[focal:, :rows] + product[:focal, rows:]).astype(out.dtype)


def respond(kept, pieces, masks, earlier):
    _, _, rows, sources = kept[0].shape
    _, per_device, _, focal, width = pieces[0].shape
    whole = pl.BlockSpec(memory_space=pltpu.VMEM)
    return pl.pallas_call(
        functools.partial(response_kernel, masks, len(kept)),
        in_specs=[whole] * (len(kept) + len(pieces)) + [pl.BlockSpec(memory_space=pl.ANY)] * len(earlier),
        out_specs=whole,
        out_shape=jax.ShapeDtypeStruct((per_device, 2, focal, rows), jnp.bfloat16),
        scratch_shapes=[pltpu.VMEM((per_device, 2 * focal, sources), jnp.bfloat16)],
        compiler_params=pltpu.CompilerParams(vmem_limit_bytes=R_VMEM),
        cost_estimate=pl.CostEstimate(flops=0, bytes_accessed=1024, transcendentals=0),
        name="respond",
    )(*kept, *pieces, *earlier)


def half_kernel(masks, last, loads, own_ref, other_ref, *refs):
    kept, (out, spectra) = refs[last : last + loads], refs[-2:]
    share, _, rows, _ = kept[0].shape
    _, bands, _, focal, width = own_ref.shape
    me = lax.axis_index("mat")
    for i in range(len(masks)):
        for core, pieces in enumerate((own_ref, other_ref)):
            start = pl.multiple_of((me % 2 ^ core) * width, width)
            spectra[i, :, :, pl.ds(start, width)] = pieces[i].reshape(bands, 2 * focal, width)
    for band in range(bands):
        total = refs[0][band] if last else None
        for i, mask in enumerate(masks):
            start = pl.multiple_of((me ^ mask) // 2 * 2 * width, 2 * width)
            part = lax.dot_general(
                kept[band // share][band % share, :, :, pl.ds(start, 2 * width)].reshape(2 * rows, 2 * width),
                spectra[i, band],
                (((1,), (1,)), ((), ())),
                preferred_element_type=jnp.float32,
            )
            total = part if total is None else total + part
        if last:
            product = total.T
            out[band, 0] = (product[:focal, :rows] - product[focal:, rows:]).astype(out.dtype)
            out[band, 1] = (product[focal:, :rows] + product[:focal, rows:]).astype(out.dtype)
        else:
            out[band] = total


def respond_half(kept, own, other, masks, before, earlier):
    _, _, rows, _ = kept[0].shape
    _, per_device, _, focal, width = own.shape
    whole = pl.BlockSpec(memory_space=pltpu.VMEM)
    if before is None:
        shape = jax.ShapeDtypeStruct((per_device, 2 * rows, 2 * focal), jnp.float32)
        given = []
    else:
        shape = jax.ShapeDtypeStruct((per_device, 2, focal, rows), jnp.bfloat16)
        given = [before]
    return pl.pallas_call(
        functools.partial(half_kernel, masks, before is not None, len(kept)),
        in_specs=[whole] * (2 + len(given) + len(kept)) + [pl.BlockSpec(memory_space=pl.ANY)] * len(earlier),
        out_specs=whole,
        out_shape=shape,
        scratch_shapes=[pltpu.VMEM((len(masks), per_device, 2 * focal, 2 * width), jnp.bfloat16)],
        compiler_params=pltpu.CompilerParams(vmem_limit_bytes=R_VMEM),
        cost_estimate=pl.CostEstimate(flops=0, bytes_accessed=1024, transcendentals=0),
        name="respond_half",
    )(own, other, *given, *kept, *earlier)


def spread_kernel(table_ref, out):
    def store(i, block):
        out[pl.ds(i * ROWS, ROWS), :] = block

    table = table_ref[1]
    wide = lax.dot_general(
        table, repeats(table.shape[0]), (((0,), (0,)), ((), ())), preferred_element_type=jnp.float32
    )
    spread_rows(store, wide)


def spread(table):
    _, count, times = table.shape
    whole = pl.BlockSpec(memory_space=pltpu.VMEM)
    return pl.pallas_call(
        spread_kernel,
        in_specs=[whole],
        out_specs=whole,
        out_shape=jax.ShapeDtypeStruct((times * ROWS, count * ROWS), jnp.bfloat16),
        compiler_params=pltpu.CompilerParams(vmem_limit_bytes=S_VMEM),
        cost_estimate=pl.CostEstimate(flops=0, bytes_accessed=2 * times * ROWS * count * ROWS, transcendentals=0),
        name="spread",
    )(table)


def inverse_kernel(first, has_before, spread, onset_ref, *refs):
    pieces, (out, weights, slots, sems) = refs[: -4 - has_before], refs[-4:]
    depth, times, rows, width = slots.shape
    cuts = sems.shape[1]
    some = times // cuts
    focal = pieces[0].shape[2]
    local_times = out.shape[0]
    steps = local_times // times
    count = steps * (focal // rows)
    share = weights.shape[0] // len(pieces)
    begin = lax.axis_index("freq") * local_times

    def send(i, cut):
        slot = lax.rem(i, depth)
        start = lax.rem(i, steps) * times + cut * some
        target = out.at[pl.ds(start, some), pl.ds(first + i // steps * rows, rows), :]
        return pltpu.make_async_copy(slots.at[slot, pl.ds(cut * some, some)], target, sems.at[slot, cut])

    @pl.loop(0, count)
    def _(i):
        step = lax.rem(i, steps)
        slot = lax.rem(i, depth)
        place = pl.ds(pl.multiple_of(i // steps * rows, rows), rows)

        @pl.when(i >= depth)
        def _():
            for cut in range(cuts):
                send(i - depth, cut).wait()

        @pl.when(step == 0)
        def _():
            for j, piece in enumerate(pieces):
                weights[pl.ds(j * share, share), :] = piece[:, :, place, :].reshape(share, width)

        onset = onset_ref[pl.ds(pl.multiple_of(first + i // steps * rows, rows), rows), :]
        for cut in range(cuts):
            start = step * times + cut * some
            lines = pl.ds(pl.multiple_of(start * rows, some * rows), some * rows)
            signal = jnp.dot(spread[lines, :], weights[...], preferred_element_type=jnp.float32)
            signal = signal.reshape(some, rows, width)
            moment = begin + start + lax.broadcasted_iota(jnp.int32, (some, 1, 1), 0)
            windowed = jnp.where(moment < onset[None], signal, 0.0).astype(out.dtype)
            slots[slot, pl.ds(cut * some, some)] = windowed
            send(i, cut).start()

    for i in range(max(0, count - depth), count):
        for cut in range(cuts):
            send(jnp.int32(i), cut).wait()


def invert(table, onset, pieces, before, first, shape):
    local_times, _, width = shape
    focal = pieces[0].shape[2]
    times = min(I_TIMES, local_times)
    has_before = before is not None
    operands = [table, onset, *pieces] + ([before] if has_before else [])
    whole = pl.BlockSpec(memory_space=pltpu.VMEM)
    anywhere = pl.BlockSpec(memory_space=pl.ANY)
    return pl.pallas_call(
        functools.partial(inverse_kernel, first, has_before),
        in_specs=[whole] * (2 + len(pieces)) + [anywhere] * has_before,
        out_specs=anywhere,
        out_shape=jax.ShapeDtypeStruct(shape, jnp.bfloat16),
        scratch_shapes=[
            pltpu.VMEM((table.shape[1], width), jnp.bfloat16),
            pltpu.VMEM((I_SLOTS, times, ROWS, width), jnp.bfloat16),
            pltpu.SemaphoreType.DMA((I_SLOTS, I_CUTS)),
        ],
        input_output_aliases={len(operands) - 1: 0} if has_before else {},
        compiler_params=pltpu.CompilerParams(vmem_limit_bytes=I_VMEM),
        cost_estimate=pl.CostEstimate(
            flops=2 * table.shape[1] * local_times * focal * width,
            bytes_accessed=2 * local_times * focal * width,
            transcendentals=0,
        ),
        name="invert",
    )(*operands)


def sum_kernel(count, *refs):
    out = refs[-1]
    total = refs[0][...]
    for part in refs[1:count]:
        total = total + part[...].astype(jnp.float32)
    out[0] = total.astype(out.dtype)


def add(parts, earlier):
    whole = pl.BlockSpec(memory_space=pltpu.VMEM)
    return pl.pallas_call(
        functools.partial(sum_kernel, len(parts)),
        in_specs=[whole] * len(parts) + [pl.BlockSpec(memory_space=pl.ANY)] * len(earlier),
        out_specs=whole,
        out_shape=jax.ShapeDtypeStruct((1, *parts[0].shape), jnp.bfloat16),
        compiler_params=pltpu.CompilerParams(vmem_limit_bytes=S_VMEM),
        name="add",
    )(*parts, *earlier)


def stack_kernel(count, *refs):
    out, place = refs[-1], 0
    for piece in refs[:count]:
        out[pl.ds(place, piece.shape[0])] = piece[...]
        place += piece.shape[0]


def stack(pieces, earlier):
    whole = pl.BlockSpec(memory_space=pltpu.VMEM)
    total = sum(piece.shape[0] for piece in pieces)
    return pl.pallas_call(
        functools.partial(stack_kernel, len(pieces)),
        in_specs=[whole] * len(pieces) + [pl.BlockSpec(memory_space=pl.ANY)] * len(earlier),
        out_specs=whole,
        out_shape=jax.ShapeDtypeStruct((total, *pieces[0].shape[1:]), pieces[0].dtype),
        compiler_params=pltpu.CompilerParams(vmem_limit_bytes=S_VMEM),
        name="stack",
    )(*pieces, *earlier)


def swap(array, axis, mask):
    return lax.ppermute(array, axis, [(i, i ^ mask) for i in range(lax.axis_size(axis))])


def on_device(traces, reflection, onset):
    local_times, focal_count, _ = traces.shape
    freq_devices, mat_devices = lax.axis_size("freq"), lax.axis_size("mat")
    per_device = reflection.shape[0]
    table = tables(per_device, freq_devices, local_times)
    focal = focal_count // CHUNKS

    steps = [1 << bit for bit in reversed(range(1, mat_devices.bit_length() - 1))]

    parts = [forward(table, traces, i * focal, focal, per_device, freq_devices) for i in range(CHUNKS)]
    spectra = []
    inverse_spread = spread(table)
    some = max(1, per_device // 2)
    kept = []
    for i, part in enumerate(parts):
        arrived = [swap(part[mask], "freq", mask) for mask in range(1, freq_devices)]
        if spectra:
            kept.append(load(reflection, 0, some, [spectra[0]]))
        spectra.append(add([part[0], *arrived], [later[0] for later in parts[i + 1 :]] or kept))
    held, masks, tied = [], [0], []
    for block in spectra:
        for step in steps[:-1]:
            block = stack([block, swap(block, "mat", step)], tied or [spectra[-1]])
        if not tied:
            tied = [load(reflection, some, per_device - some, [spectra[-1]]), inverse_spread]
        held.append((block, swap(block, "mat", steps[-1])))
    for step in steps[:-1]:
        masks = masks + [mask ^ step for mask in masks]
    masks = [masks, [mask ^ steps[-1] for mask in masks]]
    masks += [[mask ^ 1 for mask in some] for some in masks]

    kept += tied[:1]
    responses = []
    for i, (block, other) in enumerate(held):
        beside = swap(block, "mat", 1)
        if responses:
            half = respond_half(kept, block, beside, masks[0], None, [responses[-1][0]])
            other = stack([other], [half])
            response = respond_half(kept, other, swap(other, "mat", 1), masks[1], half, [])
        else:
            pieces = [block, other, beside, swap(other, "mat", 1)]
            response = respond(kept, pieces, masks, [later for later, _ in held[i + 1 :]])
        responses.append([response] + [swap(response, "freq", mask) for mask in range(1, freq_devices)])
    windowed = None
    for i, pieces in enumerate(responses):
        windowed = invert(inverse_spread, onset, pieces, windowed, i * focal, traces.shape)
    return windowed


def solution(mesh):
    placed = (P("freq", None, "mat"), P("freq", None, "mat", None), P(None, "mat"))
    return jax.shard_map(
        on_device, mesh=mesh, in_specs=placed, out_specs=P("freq", None, "mat"), check_vma=False
    )
```

```python
import functools
import math

import jax
import jax.numpy as jnp
from jax import lax
from jax.experimental import pallas as pl
from jax.experimental.pallas import tpu as pltpu
from jax.sharding import PartitionSpec as P

ROWS = 16
CHUNKS = 2
F_TIMES = 128
F_SLOTS = 4
I_TIMES = 256
I_SLOTS = 2
I_CUTS = 8
MIB = 1024 * 1024
F_VMEM = 40 * MIB
R_VMEM = 12 * MIB
I_VMEM = 20 * MIB
S_VMEM = 16 * MIB
L_VMEM = 32 * MIB


def phases(bands, times, samples):
    return (bands * times % samples).astype(jnp.float32) * (2.0 * math.pi / samples)


def tables(per_device, freq_devices, local_times):
    me = lax.axis_index("freq")
    samples = local_times * freq_devices
    owners = me ^ jnp.arange(freq_devices, dtype=jnp.int32)
    bands = samples // 16 + (owners[:, None] * per_device + jnp.arange(per_device, dtype=jnp.int32)).reshape(-1)
    times = me * local_times + jnp.arange(local_times, dtype=jnp.int32)
    angles = phases(bands[:, None], times[None, :], samples)
    parts = jnp.stack([jnp.cos(angles), -jnp.sin(angles)], axis=1).reshape(-1, local_times)
    factors = (1.0 / math.sqrt(samples), 1.0 / math.sqrt(per_device * freq_devices))
    return jnp.stack([parts * factor for factor in factors]).astype(jnp.bfloat16)


def repeats(count):
    lane = lax.broadcasted_iota(jnp.int32, (count, count * ROWS), 1)
    row = lax.broadcasted_iota(jnp.int32, (count, count * ROWS), 0)
    return jnp.where(lane // ROWS == row, 1.0, 0.0).astype(jnp.bfloat16)


def spread_rows(store, wide):
    lane = lax.broadcasted_iota(jnp.int32, (ROWS, wide.shape[1]), 1)
    row = lax.broadcasted_iota(jnp.int32, (ROWS, wide.shape[1]), 0)
    own = lane % ROWS == row
    for i in range(wide.shape[0]):
        store(i, jnp.where(own, wide[i : i + 1], 0.0).astype(jnp.bfloat16))


def forward_kernel(first, focal, table_ref, traces_ref, *refs):
    *outs, spread, total, slots, sems = refs
    depth, times, rows, width = slots.shape
    steps = spread.shape[0]
    count = steps * (focal // rows)

    def fetch(i):
        source = traces_ref.at[pl.ds(i % steps * times, times), pl.ds(first + i // steps * rows, rows), :]
        return pltpu.make_async_copy(source, slots.at[i % depth], sems.at[i % depth])

    for i in range(min(depth - 1, count)):
        fetch(i).start()

    for step in range(steps):

        def store(i, block, step=step):
            spread[step, pl.ds(i * rows, rows), :] = block

        some = table_ref[0, :, pl.ds(step * times, times)]
        spread_rows(store, jnp.dot(some, repeats(times), preferred_element_type=jnp.float32))

    for i in range(count):
        if i + depth - 1 < count:
            fetch(i + depth - 1).start()
        fetch(i).wait()
        step = i % steps
        block = slots[i % depth].reshape(times * rows, width)
        part = jnp.dot(spread[step], block, preferred_element_type=jnp.float32)
        if step > 0:
            part = total[...] + part
        if step < steps - 1:
            total[...] = part
            continue
        share = total.shape[0] // len(outs)
        place = pl.ds(i // steps * rows, rows)
        for j, out in enumerate(outs):
            value = part[j * share : (j + 1) * share].reshape(*out.shape[:2], rows, width)
            out[:, :, place, :] = value.astype(out.dtype)


def forward(table, traces, first, focal, per_device, freq_devices):
    local_times, _, width = traces.shape
    times = min(F_TIMES, local_times)
    steps = local_times // times
    count = 2 * per_device * freq_devices
    shape = (per_device, 2, focal, width)
    whole = pl.BlockSpec(memory_space=pltpu.VMEM)
    return pl.pallas_call(
        functools.partial(forward_kernel, first, focal),
        in_specs=[whole, pl.BlockSpec(memory_space=pl.ANY)],
        out_specs=[whole] * freq_devices,
        out_shape=[jax.ShapeDtypeStruct(shape, jnp.float32 if i == 0 else jnp.bfloat16) for i in range(freq_devices)],
        scratch_shapes=[
            pltpu.VMEM((steps, count * ROWS, times * ROWS), jnp.bfloat16),
            pltpu.VMEM((count * ROWS, width), jnp.float32),
            pltpu.VMEM((F_SLOTS, times, ROWS, width), jnp.bfloat16),
            pltpu.SemaphoreType.DMA((F_SLOTS,)),
        ],
        compiler_params=pltpu.CompilerParams(vmem_limit_bytes=F_VMEM),
        cost_estimate=pl.CostEstimate(
            flops=2 * count * ROWS * local_times * focal * width,
            bytes_accessed=2 * local_times * focal * width,
            transcendentals=0,
        ),
        name="forward",
    )(table, traces)


def load_kernel(first, reflection_ref, *refs):
    out, sems = refs[-2:]
    bands, parts = out.shape[:2]

    def fetch(band, part):
        return pltpu.make_async_copy(reflection_ref.at[first + band, part], out.at[band, part], sems.at[band, part])

    for band in range(bands):
        for part in range(parts):
            fetch(band, part).start()
    for band in range(bands):
        for part in range(parts):
            fetch(band, part).wait()


def load(reflection, first, bands, earlier):
    return pl.pallas_call(
        functools.partial(load_kernel, first),
        in_specs=[pl.BlockSpec(memory_space=pl.ANY)] * (1 + len(earlier)),
        out_specs=pl.BlockSpec(memory_space=pltpu.VMEM),
        out_shape=jax.ShapeDtypeStruct((bands, *reflection.shape[1:]), reflection.dtype),
        scratch_shapes=[pltpu.SemaphoreType.DMA((bands, reflection.shape[1]))],
        compiler_params=pltpu.CompilerParams(vmem_limit_bytes=L_VMEM),
        name="load",
    )(reflection, *earlier)


def response_kernel(masks, loads, *refs):
    kept, refs = refs[:loads], refs[loads:]
    out, spectra = refs[-2:]
    share, _, rows, sources = kept[0].shape
    _, bands, _, focal, width = refs[0].shape
    me = lax.axis_index("mat")
    for pieces, origins in zip(refs, masks):
        for i, mask in enumerate(origins):
            start = pl.multiple_of((me ^ mask) * width, width)
            spectra[:, :, pl.ds(start, width)] = pieces[i].reshape(bands, 2 * focal, width)
    for band in range(bands):
        product = lax.dot_general(
            kept[band // share][band % share].reshape(2 * rows, sources),
            spectra[band],
            (((1,), (1,)), ((), ())),
            preferred_element_type=jnp.float32,
        ).T
        out[band, 0] = (product[:focal, :rows] - product[focal:, rows:]).astype(out.dtype)
        out[band, 1] = (product[focal:, :rows] + product[:focal, rows:]).astype(out.dtype)


def respond(kept, pieces, masks, earlier):
    _, _, rows, sources = kept[0].shape
    _, per_device, _, focal, width = pieces[0].shape
    whole = pl.BlockSpec(memory_space=pltpu.VMEM)
    return pl.pallas_call(
        functools.partial(response_kernel, masks, len(kept)),
        in_specs=[whole] * (len(kept) + len(pieces)) + [pl.BlockSpec(memory_space=pl.ANY)] * len(earlier),
        out_specs=whole,
        out_shape=jax.ShapeDtypeStruct((per_device, 2, focal, rows), jnp.bfloat16),
        scratch_shapes=[pltpu.VMEM((per_device, 2 * focal, sources), jnp.bfloat16)],
        compiler_params=pltpu.CompilerParams(vmem_limit_bytes=R_VMEM),
        cost_estimate=pl.CostEstimate(flops=0, bytes_accessed=1024, transcendentals=0),
        name="respond",
    )(*kept, *pieces, *earlier)


def half_kernel(masks, last, loads, own_ref, other_ref, *refs):
    kept, (out, spectra) = refs[last : last + loads], refs[-2:]
    share, _, rows, _ = kept[0].shape
    _, bands, _, focal, width = own_ref.shape
    me = lax.axis_index("mat")
    for i in range(len(masks)):
        for core, pieces in enumerate((own_ref, other_ref)):
            start = pl.multiple_of((me % 2 ^ core) * width, width)
            spectra[i, :, :, pl.ds(start, width)] = pieces[i].reshape(bands, 2 * focal, width)
    for band in range(bands):
        total = refs[0][band] if last else None
        for i, mask in enumerate(masks):
            start = pl.multiple_of((me ^ mask) // 2 * 2 * width, 2 * width)
            part = lax.dot_general(
                kept[band // share][band % share, :, :, pl.ds(start, 2 * width)].reshape(2 * rows, 2 * width),
                spectra[i, band],
                (((1,), (1,)), ((), ())),
                preferred_element_type=jnp.float32,
            )
            total = part if total is None else total + part
        if last:
            product = total.T
            out[band, 0] = (product[:focal, :rows] - product[focal:, rows:]).astype(out.dtype)
            out[band, 1] = (product[focal:, :rows] + product[:focal, rows:]).astype(out.dtype)
        else:
            out[band] = total


def respond_half(kept, own, other, masks, before, earlier):
    _, _, rows, _ = kept[0].shape
    _, per_device, _, focal, width = own.shape
    whole = pl.BlockSpec(memory_space=pltpu.VMEM)
    if before is None:
        shape = jax.ShapeDtypeStruct((per_device, 2 * rows, 2 * focal), jnp.float32)
        given = []
    else:
        shape = jax.ShapeDtypeStruct((per_device, 2, focal, rows), jnp.bfloat16)
        given = [before]
    return pl.pallas_call(
        functools.partial(half_kernel, masks, before is not None, len(kept)),
        in_specs=[whole] * (2 + len(given) + len(kept)) + [pl.BlockSpec(memory_space=pl.ANY)] * len(earlier),
        out_specs=whole,
        out_shape=shape,
        scratch_shapes=[pltpu.VMEM((len(masks), per_device, 2 * focal, 2 * width), jnp.bfloat16)],
        compiler_params=pltpu.CompilerParams(vmem_limit_bytes=R_VMEM),
        cost_estimate=pl.CostEstimate(flops=0, bytes_accessed=1024, transcendentals=0),
        name="respond_half",
    )(own, other, *given, *kept, *earlier)


def spread_kernel(table_ref, out):
    def store(i, block):
        out[pl.ds(i * ROWS, ROWS), :] = block

    table = table_ref[1]
    wide = lax.dot_general(
        table, repeats(table.shape[0]), (((0,), (0,)), ((), ())), preferred_element_type=jnp.float32
    )
    spread_rows(store, wide)


def spread(table):
    _, count, times = table.shape
    whole = pl.BlockSpec(memory_space=pltpu.VMEM)
    return pl.pallas_call(
        spread_kernel,
        in_specs=[whole],
        out_specs=whole,
        out_shape=jax.ShapeDtypeStruct((times * ROWS, count * ROWS), jnp.bfloat16),
        compiler_params=pltpu.CompilerParams(vmem_limit_bytes=S_VMEM),
        cost_estimate=pl.CostEstimate(flops=0, bytes_accessed=2 * times * ROWS * count * ROWS, transcendentals=0),
        name="spread",
    )(table)


def inverse_kernel(first, has_before, spread, onset_ref, *refs):
    pieces, (out, weights, slots, sems) = refs[: -4 - has_before], refs[-4:]
    depth, times, rows, width = slots.shape
    cuts = sems.shape[1]
    some = times // cuts
    focal = pieces[0].shape[2]
    local_times = out.shape[0]
    steps = local_times // times
    count = steps * (focal // rows)
    share = weights.shape[0] // len(pieces)
    begin = lax.axis_index("freq") * local_times

    def send(i, cut):
        slot = lax.rem(i, depth)
        start = lax.rem(i, steps) * times + cut * some
        target = out.at[pl.ds(start, some), pl.ds(first + i // steps * rows, rows), :]
        return pltpu.make_async_copy(slots.at[slot, pl.ds(cut * some, some)], target, sems.at[slot, cut])

    @pl.loop(0, count)
    def _(i):
        step = lax.rem(i, steps)
        slot = lax.rem(i, depth)
        place = pl.ds(pl.multiple_of(i // steps * rows, rows), rows)

        @pl.when(i >= depth)
        def _():
            for cut in range(cuts):
                send(i - depth, cut).wait()

        @pl.when(step == 0)
        def _():
            for j, piece in enumerate(pieces):
                weights[pl.ds(j * share, share), :] = piece[:, :, place, :].reshape(share, width)

        onset = onset_ref[pl.ds(pl.multiple_of(first + i // steps * rows, rows), rows), :]
        for cut in range(cuts):
            start = step * times + cut * some
            lines = pl.ds(pl.multiple_of(start * rows, some * rows), some * rows)
            signal = jnp.dot(spread[lines, :], weights[...], preferred_element_type=jnp.float32)
            signal = signal.reshape(some, rows, width)
            moment = begin + start + lax.broadcasted_iota(jnp.int32, (some, 1, 1), 0)
            windowed = jnp.where(moment < onset[None], signal, 0.0).astype(out.dtype)
            slots[slot, pl.ds(cut * some, some)] = windowed
            send(i, cut).start()

    for i in range(max(0, count - depth), count):
        for cut in range(cuts):
            send(jnp.int32(i), cut).wait()


def invert(table, onset, pieces, before, first, shape):
    local_times, _, width = shape
    focal = pieces[0].shape[2]
    times = min(I_TIMES, local_times)
    has_before = before is not None
    operands = [table, onset, *pieces] + ([before] if has_before else [])
    whole = pl.BlockSpec(memory_space=pltpu.VMEM)
    anywhere = pl.BlockSpec(memory_space=pl.ANY)
    return pl.pallas_call(
        functools.partial(inverse_kernel, first, has_before),
        in_specs=[whole] * (2 + len(pieces)) + [anywhere] * has_before,
        out_specs=anywhere,
        out_shape=jax.ShapeDtypeStruct(shape, jnp.bfloat16),
        scratch_shapes=[
            pltpu.VMEM((table.shape[1], width), jnp.bfloat16),
            pltpu.VMEM((I_SLOTS, times, ROWS, width), jnp.bfloat16),
            pltpu.SemaphoreType.DMA((I_SLOTS, I_CUTS)),
        ],
        input_output_aliases={len(operands) - 1: 0} if has_before else {},
        compiler_params=pltpu.CompilerParams(vmem_limit_bytes=I_VMEM),
        cost_estimate=pl.CostEstimate(
            flops=2 * table.shape[1] * local_times * focal * width,
            bytes_accessed=2 * local_times * focal * width,
            transcendentals=0,
        ),
        name="invert",
    )(*operands)


def sum_kernel(count, *refs):
    out = refs[-1]
    total = refs[0][...]
    for part in refs[1:count]:
        total = total + part[...].astype(jnp.float32)
    out[0] = total.astype(out.dtype)


def add(parts, earlier):
    whole = pl.BlockSpec(memory_space=pltpu.VMEM)
    return pl.pallas_call(
        functools.partial(sum_kernel, len(parts)),
        in_specs=[whole] * len(parts) + [pl.BlockSpec(memory_space=pl.ANY)] * len(earlier),
        out_specs=whole,
        out_shape=jax.ShapeDtypeStruct((1, *parts[0].shape), jnp.bfloat16),
        compiler_params=pltpu.CompilerParams(vmem_limit_bytes=S_VMEM),
        name="add",
    )(*parts, *earlier)


def stack_kernel(count, *refs):
    out, place = refs[-1], 0
    for piece in refs[:count]:
        out[pl.ds(place, piece.shape[0])] = piece[...]
        place += piece.shape[0]


def stack(pieces, earlier):
    whole = pl.BlockSpec(memory_space=pltpu.VMEM)
    total = sum(piece.shape[0] for piece in pieces)
    return pl.pallas_call(
        functools.partial(stack_kernel, len(pieces)),
        in_specs=[whole] * len(pieces) + [pl.BlockSpec(memory_space=pl.ANY)] * len(earlier),
        out_specs=whole,
        out_shape=jax.ShapeDtypeStruct((total, *pieces[0].shape[1:]), pieces[0].dtype),
        compiler_params=pltpu.CompilerParams(vmem_limit_bytes=S_VMEM),
        name="stack",
    )(*pieces, *earlier)


def swap(array, axis, mask):
    return lax.ppermute(array, axis, [(i, i ^ mask) for i in range(lax.axis_size(axis))])


def on_device(traces, reflection, onset):
    local_times, focal_count, _ = traces.shape
    freq_devices, mat_devices = lax.axis_size("freq"), lax.axis_size("mat")
    per_device = reflection.shape[0]
    table = tables(per_device, freq_devices, local_times)
    focal = focal_count // CHUNKS

    steps = [1 << bit for bit in reversed(range(1, mat_devices.bit_length() - 1))]

    parts = [forward(table, traces, i * focal, focal, per_device, freq_devices) for i in range(CHUNKS)]
    spectra = []
    inverse_spread = spread(table)
    some = max(1, per_device // 2)
    kept = []
    for i, part in enumerate(parts):
        arrived = [swap(part[mask], "freq", mask) for mask in range(1, freq_devices)]
        if spectra:
            kept.append(load(reflection, 0, some, [spectra[0]]))
        spectra.append(add([part[0], *arrived], [later[0] for later in parts[i + 1 :]] or kept))
    held, masks, tied = [], [0], []
    for block in spectra:
        for step in steps[:-1]:
            block = stack([block, swap(block, "mat", step)], tied or [spectra[-1]])
        if not tied:
            tied = [load(reflection, some, per_device - some, [spectra[-1]]), inverse_spread]
        held.append((block, swap(block, "mat", steps[-1])))
    for step in steps[:-1]:
        masks = masks + [mask ^ step for mask in masks]
    masks = [masks, [mask ^ steps[-1] for mask in masks]]
    masks += [[mask ^ 1 for mask in some] for some in masks]

    kept += tied[:1]
    responses = []
    for i, (block, other) in enumerate(held):
        beside = swap(block, "mat", 1)
        if responses:
            half = respond_half(kept, block, beside, masks[0], None, [responses[-1][0]])
            other = stack([other], [half])
            response = respond_half(kept, other, swap(other, "mat", 1), masks[1], half, [])
        else:
            pieces = [block, other, beside, swap(other, "mat", 1)]
            response = respond(kept, pieces, masks, [later for later, _ in held[i + 1 :]])
        responses.append([response] + [swap(response, "freq", mask) for mask in range(1, freq_devices)])
    windowed = None
    for i, pieces in enumerate(responses):
        windowed = invert(inverse_spread, onset, pieces, windowed, i * focal, traces.shape)
    return windowed


def solution(mesh):
    placed = (P("freq", None, "mat"), P("freq", None, "mat", None), P(None, "mat"))
    return jax.shard_map(
        on_device, mesh=mesh, in_specs=placed, out_specs=P("freq", None, "mat"), check_vma=False
    )
```

```python
import functools
import math

import jax
import jax.numpy as jnp
from jax import lax
from jax.experimental import pallas as pl
from jax.experimental.pallas import tpu as pltpu
from jax.sharding import PartitionSpec as P

ROWS = 16
CHUNKS = 2
F_TIMES = 64
F_SLOTS = 8
I_TIMES = 256
I_SLOTS = 2
I_CUTS = 8
MIB = 1024 * 1024
F_VMEM = 40 * MIB
R_VMEM = 12 * MIB
I_VMEM = 20 * MIB
S_VMEM = 16 * MIB
L_VMEM = 32 * MIB


def phases(bands, times, samples):
    return (bands * times % samples).astype(jnp.float32) * (2.0 * math.pi / samples)


def tables(per_device, freq_devices, local_times):
    me = lax.axis_index("freq")
    samples = local_times * freq_devices
    owners = me ^ jnp.arange(freq_devices, dtype=jnp.int32)
    bands = samples // 16 + (owners[:, None] * per_device + jnp.arange(per_device, dtype=jnp.int32)).reshape(-1)
    times = me * local_times + jnp.arange(local_times, dtype=jnp.int32)
    angles = phases(bands[:, None], times[None, :], samples)
    parts = jnp.stack([jnp.cos(angles), -jnp.sin(angles)], axis=1).reshape(-1, local_times)
    factors = (1.0 / math.sqrt(samples), 1.0 / math.sqrt(per_device * freq_devices))
    return jnp.stack([parts * factor for factor in factors]).astype(jnp.bfloat16)


def repeats(count):
    lane = lax.broadcasted_iota(jnp.int32, (count, count * ROWS), 1)
    row = lax.broadcasted_iota(jnp.int32, (count, count * ROWS), 0)
    return jnp.where(lane // ROWS == row, 1.0, 0.0).astype(jnp.bfloat16)


def spread_rows(store, wide):
    lane = lax.broadcasted_iota(jnp.int32, (ROWS, wide.shape[1]), 1)
    row = lax.broadcasted_iota(jnp.int32, (ROWS, wide.shape[1]), 0)
    own = lane % ROWS == row
    for i in range(wide.shape[0]):
        store(i, jnp.where(own, wide[i : i + 1], 0.0).astype(jnp.bfloat16))


def forward_kernel(first, focal, table_ref, traces_ref, *refs):
    *outs, spread, total, slots, sems = refs
    depth, times, rows, width = slots.shape
    steps = spread.shape[0]
    count = steps * (focal // rows)

    def fetch(i):
        source = traces_ref.at[pl.ds(i % steps * times, times), pl.ds(first + i // steps * rows, rows), :]
        return pltpu.make_async_copy(source, slots.at[i % depth], sems.at[i % depth])

    for i in range(min(depth - 1, count)):
        fetch(i).start()

    for step in range(steps):

        def store(i, block, step=step):
            spread[step, pl.ds(i * rows, rows), :] = block

        some = table_ref[0, :, pl.ds(step * times, times)]
        spread_rows(store, jnp.dot(some, repeats(times), preferred_element_type=jnp.float32))

    for i in range(count):
        if i + depth - 1 < count:
            fetch(i + depth - 1).start()
        fetch(i).wait()
        step = i % steps
        block = slots[i % depth].reshape(times * rows, width)
        part = jnp.dot(spread[step], block, preferred_element_type=jnp.float32)
        if step > 0:
            part = total[...] + part
        if step < steps - 1:
            total[...] = part
            continue
        share = total.shape[0] // len(outs)
        place = pl.ds(i // steps * rows, rows)
        for j, out in enumerate(outs):
            value = part[j * share : (j + 1) * share].reshape(*out.shape[:2], rows, width)
            out[:, :, place, :] = value.astype(out.dtype)


def forward(table, traces, first, focal, per_device, freq_devices):
    local_times, _, width = traces.shape
    times = min(F_TIMES, local_times)
    steps = local_times // times
    count = 2 * per_device * freq_devices
    shape = (per_device, 2, focal, width)
    whole = pl.BlockSpec(memory_space=pltpu.VMEM)
    return pl.pallas_call(
        functools.partial(forward_kernel, first, focal),
        in_specs=[whole, pl.BlockSpec(memory_space=pl.ANY)],
        out_specs=[whole] * freq_devices,
        out_shape=[jax.ShapeDtypeStruct(shape, jnp.float32 if i == 0 else jnp.bfloat16) for i in range(freq_devices)],
        scratch_shapes=[
            pltpu.VMEM((steps, count * ROWS, times * ROWS), jnp.bfloat16),
            pltpu.VMEM((count * ROWS, width), jnp.float32),
            pltpu.VMEM((F_SLOTS, times, ROWS, width), jnp.bfloat16),
            pltpu.SemaphoreType.DMA((F_SLOTS,)),
        ],
        compiler_params=pltpu.CompilerParams(vmem_limit_bytes=F_VMEM),
        cost_estimate=pl.CostEstimate(
            flops=2 * count * ROWS * local_times * focal * width,
            bytes_accessed=2 * local_times * focal * width,
            transcendentals=0,
        ),
        name="forward",
    )(table, traces)


def load_kernel(first, reflection_ref, *refs):
    out, sems = refs[-2:]
    bands, parts = out.shape[:2]

    def fetch(band, part):
        return pltpu.make_async_copy(reflection_ref.at[first + band, part], out.at[band, part], sems.at[band, part])

    for band in range(bands):
        for part in range(parts):
            fetch(band, part).start()
    for band in range(bands):
        for part in range(parts):
            fetch(band, part).wait()


def load(reflection, first, bands, earlier):
    return pl.pallas_call(
        functools.partial(load_kernel, first),
        in_specs=[pl.BlockSpec(memory_space=pl.ANY)] * (1 + len(earlier)),
        out_specs=pl.BlockSpec(memory_space=pltpu.VMEM),
        out_shape=jax.ShapeDtypeStruct((bands, *reflection.shape[1:]), reflection.dtype),
        scratch_shapes=[pltpu.SemaphoreType.DMA((bands, reflection.shape[1]))],
        compiler_params=pltpu.CompilerParams(vmem_limit_bytes=L_VMEM),
        name="load",
    )(reflection, *earlier)


def response_kernel(masks, loads, *refs):
    kept, refs = refs[:loads], refs[loads:]
    out, spectra = refs[-2:]
    share, _, rows, sources = kept[0].shape
    _, bands, _, focal, width = refs[0].shape
    me = lax.axis_index("mat")
    for pieces, origins in zip(refs, masks):
        for i, mask in enumerate(origins):
            start = pl.multiple_of((me ^ mask) * width, width)
            spectra[:, :, pl.ds(start, width)] = pieces[i].reshape(bands, 2 * focal, width)
    for band in range(bands):
        product = lax.dot_general(
            kept[band // share][band % share].reshape(2 * rows, sources),
            spectra[band],
            (((1,), (1,)), ((), ())),
            preferred_element_type=jnp.float32,
        ).T
        out[band, 0] = (product[:focal, :rows] - product[focal:, rows:]).astype(out.dtype)
        out[band, 1] = (product[focal:, :rows] + product[:focal, rows:]).astype(out.dtype)


def respond(kept, pieces, masks, earlier):
    _, _, rows, sources = kept[0].shape
    _, per_device, _, focal, width = pieces[0].shape
    whole = pl.BlockSpec(memory_space=pltpu.VMEM)
    return pl.pallas_call(
        functools.partial(response_kernel, masks, len(kept)),
        in_specs=[whole] * (len(kept) + len(pieces)) + [pl.BlockSpec(memory_space=pl.ANY)] * len(earlier),
        out_specs=whole,
        out_shape=jax.ShapeDtypeStruct((per_device, 2, focal, rows), jnp.bfloat16),
        scratch_shapes=[pltpu.VMEM((per_device, 2 * focal, sources), jnp.bfloat16)],
        compiler_params=pltpu.CompilerParams(vmem_limit_bytes=R_VMEM),
        cost_estimate=pl.CostEstimate(flops=0, bytes_accessed=1024, transcendentals=0),
        name="respond",
    )(*kept, *pieces, *earlier)


def half_kernel(masks, last, loads, own_ref, other_ref, *refs):
    kept, (out, spectra) = refs[last : last + loads], refs[-2:]
    share, _, rows, _ = kept[0].shape
    _, bands, _, focal, width = own_ref.shape
    me = lax.axis_index("mat")
    for i in range(len(masks)):
        for core, pieces in enumerate((own_ref, other_ref)):
            start = pl.multiple_of((me % 2 ^ core) * width, width)
            spectra[i, :, :, pl.ds(start, width)] = pieces[i].reshape(bands, 2 * focal, width)
    for band in range(bands):
        total = refs[0][band] if last else None
        for i, mask in enumerate(masks):
            start = pl.multiple_of((me ^ mask) // 2 * 2 * width, 2 * width)
            part = lax.dot_general(
                kept[band // share][band % share, :, :, pl.ds(start, 2 * width)].reshape(2 * rows, 2 * width),
                spectra[i, band],
                (((1,), (1,)), ((), ())),
                preferred_element_type=jnp.float32,
            )
            total = part if total is None else total + part
        if last:
            product = total.T
            out[band, 0] = (product[:focal, :rows] - product[focal:, rows:]).astype(out.dtype)
            out[band, 1] = (product[focal:, :rows] + product[:focal, rows:]).astype(out.dtype)
        else:
            out[band] = total


def respond_half(kept, own, other, masks, before, earlier):
    _, _, rows, _ = kept[0].shape
    _, per_device, _, focal, width = own.shape
    whole = pl.BlockSpec(memory_space=pltpu.VMEM)
    if before is None:
        shape = jax.ShapeDtypeStruct((per_device, 2 * rows, 2 * focal), jnp.float32)
        given = []
    else:
        shape = jax.ShapeDtypeStruct((per_device, 2, focal, rows), jnp.bfloat16)
        given = [before]
    return pl.pallas_call(
        functools.partial(half_kernel, masks, before is not None, len(kept)),
        in_specs=[whole] * (2 + len(given) + len(kept)) + [pl.BlockSpec(memory_space=pl.ANY)] * len(earlier),
        out_specs=whole,
        out_shape=shape,
        scratch_shapes=[pltpu.VMEM((len(masks), per_device, 2 * focal, 2 * width), jnp.bfloat16)],
        compiler_params=pltpu.CompilerParams(vmem_limit_bytes=R_VMEM),
        cost_estimate=pl.CostEstimate(flops=0, bytes_accessed=1024, transcendentals=0),
        name="respond_half",
    )(own, other, *given, *kept, *earlier)


def spread_kernel(table_ref, out):
    def store(i, block):
        out[pl.ds(i * ROWS, ROWS), :] = block

    table = table_ref[1]
    wide = lax.dot_general(
        table, repeats(table.shape[0]), (((0,), (0,)), ((), ())), preferred_element_type=jnp.float32
    )
    spread_rows(store, wide)


def spread(table):
    _, count, times = table.shape
    whole = pl.BlockSpec(memory_space=pltpu.VMEM)
    return pl.pallas_call(
        spread_kernel,
        in_specs=[whole],
        out_specs=whole,
        out_shape=jax.ShapeDtypeStruct((times * ROWS, count * ROWS), jnp.bfloat16),
        compiler_params=pltpu.CompilerParams(vmem_limit_bytes=S_VMEM),
        cost_estimate=pl.CostEstimate(flops=0, bytes_accessed=2 * times * ROWS * count * ROWS, transcendentals=0),
        name="spread",
    )(table)


def inverse_kernel(first, has_before, spread, onset_ref, *refs):
    pieces, (out, weights, slots, sems) = refs[: -4 - has_before], refs[-4:]
    depth, times, rows, width = slots.shape
    cuts = sems.shape[1]
    some = times // cuts
    focal = pieces[0].shape[2]
    local_times = out.shape[0]
    steps = local_times // times
    count = steps * (focal // rows)
    share = weights.shape[0] // len(pieces)
    begin = lax.axis_index("freq") * local_times

    def send(i, cut):
        slot = lax.rem(i, depth)
        start = lax.rem(i, steps) * times + cut * some
        target = out.at[pl.ds(start, some), pl.ds(first + i // steps * rows, rows), :]
        return pltpu.make_async_copy(slots.at[slot, pl.ds(cut * some, some)], target, sems.at[slot, cut])

    @pl.loop(0, count)
    def _(i):
        step = lax.rem(i, steps)
        slot = lax.rem(i, depth)
        place = pl.ds(pl.multiple_of(i // steps * rows, rows), rows)

        @pl.when(i >= depth)
        def _():
            for cut in range(cuts):
                send(i - depth, cut).wait()

        @pl.when(step == 0)
        def _():
            for j, piece in enumerate(pieces):
                weights[pl.ds(j * share, share), :] = piece[:, :, place, :].reshape(share, width)

        onset = onset_ref[pl.ds(pl.multiple_of(first + i // steps * rows, rows), rows), :]
        for cut in range(cuts):
            start = step * times + cut * some
            lines = pl.ds(pl.multiple_of(start * rows, some * rows), some * rows)
            signal = jnp.dot(spread[lines, :], weights[...], preferred_element_type=jnp.float32)
            signal = signal.reshape(some, rows, width)
            moment = begin + start + lax.broadcasted_iota(jnp.int32, (some, 1, 1), 0)
            windowed = jnp.where(moment < onset[None], signal, 0.0).astype(out.dtype)
            slots[slot, pl.ds(cut * some, some)] = windowed
            send(i, cut).start()

    for i in range(max(0, count - depth), count):
        for cut in range(cuts):
            send(jnp.int32(i), cut).wait()


def invert(table, onset, pieces, before, first, shape):
    local_times, _, width = shape
    focal = pieces[0].shape[2]
    times = min(I_TIMES, local_times)
    has_before = before is not None
    operands = [table, onset, *pieces] + ([before] if has_before else [])
    whole = pl.BlockSpec(memory_space=pltpu.VMEM)
    anywhere = pl.BlockSpec(memory_space=pl.ANY)
    return pl.pallas_call(
        functools.partial(inverse_kernel, first, has_before),
        in_specs=[whole] * (2 + len(pieces)) + [anywhere] * has_before,
        out_specs=anywhere,
        out_shape=jax.ShapeDtypeStruct(shape, jnp.bfloat16),
        scratch_shapes=[
            pltpu.VMEM((table.shape[1], width), jnp.bfloat16),
            pltpu.VMEM((I_SLOTS, times, ROWS, width), jnp.bfloat16),
            pltpu.SemaphoreType.DMA((I_SLOTS, I_CUTS)),
        ],
        input_output_aliases={len(operands) - 1: 0} if has_before else {},
        compiler_params=pltpu.CompilerParams(vmem_limit_bytes=I_VMEM),
        cost_estimate=pl.CostEstimate(
            flops=2 * table.shape[1] * local_times * focal * width,
            bytes_accessed=2 * local_times * focal * width,
            transcendentals=0,
        ),
        name="invert",
    )(*operands)


def sum_kernel(count, *refs):
    out = refs[-1]
    total = refs[0][...]
    for part in refs[1:count]:
        total = total + part[...].astype(jnp.float32)
    out[0] = total.astype(out.dtype)


def add(parts, earlier):
    whole = pl.BlockSpec(memory_space=pltpu.VMEM)
    return pl.pallas_call(
        functools.partial(sum_kernel, len(parts)),
        in_specs=[whole] * len(parts) + [pl.BlockSpec(memory_space=pl.ANY)] * len(earlier),
        out_specs=whole,
        out_shape=jax.ShapeDtypeStruct((1, *parts[0].shape), jnp.bfloat16),
        compiler_params=pltpu.CompilerParams(vmem_limit_bytes=S_VMEM),
        name="add",
    )(*parts, *earlier)


def stack_kernel(count, *refs):
    out, place = refs[-1], 0
    for piece in refs[:count]:
        out[pl.ds(place, piece.shape[0])] = piece[...]
        place += piece.shape[0]


def stack(pieces, earlier):
    whole = pl.BlockSpec(memory_space=pltpu.VMEM)
    total = sum(piece.shape[0] for piece in pieces)
    return pl.pallas_call(
        functools.partial(stack_kernel, len(pieces)),
        in_specs=[whole] * len(pieces) + [pl.BlockSpec(memory_space=pl.ANY)] * len(earlier),
        out_specs=whole,
        out_shape=jax.ShapeDtypeStruct((total, *pieces[0].shape[1:]), pieces[0].dtype),
        compiler_params=pltpu.CompilerParams(vmem_limit_bytes=S_VMEM),
        name="stack",
    )(*pieces, *earlier)


def swap(array, axis, mask):
    return lax.ppermute(array, axis, [(i, i ^ mask) for i in range(lax.axis_size(axis))])


def on_device(traces, reflection, onset):
    local_times, focal_count, _ = traces.shape
    freq_devices, mat_devices = lax.axis_size("freq"), lax.axis_size("mat")
    per_device = reflection.shape[0]
    table = tables(per_device, freq_devices, local_times)
    focal = focal_count // CHUNKS

    steps = [1 << bit for bit in reversed(range(1, mat_devices.bit_length() - 1))]

    parts = [forward(table, traces, i * focal, focal, per_device, freq_devices) for i in range(CHUNKS)]
    spectra = []
    inverse_spread = spread(table)
    some = max(1, per_device // 2)
    kept = []
    for i, part in enumerate(parts):
        arrived = [swap(part[mask], "freq", mask) for mask in range(1, freq_devices)]
        if spectra:
            kept.append(load(reflection, 0, some, [spectra[0]]))
        spectra.append(add([part[0], *arrived], [later[0] for later in parts[i + 1 :]] or kept))
    held, masks, tied = [], [0], []
    for block in spectra:
        for step in steps[:-1]:
            block = stack([block, swap(block, "mat", step)], tied or [spectra[-1]])
        if not tied:
            tied = [load(reflection, some, per_device - some, [spectra[-1]]), inverse_spread]
        held.append((block, swap(block, "mat", steps[-1])))
    for step in steps[:-1]:
        masks = masks + [mask ^ step for mask in masks]
    masks = [masks, [mask ^ steps[-1] for mask in masks]]
    masks += [[mask ^ 1 for mask in some] for some in masks]

    kept += tied[:1]
    responses = []
    for i, (block, other) in enumerate(held):
        beside = swap(block, "mat", 1)
        if responses:
            half = respond_half(kept, block, beside, masks[0], None, [responses[-1][0]])
            other = stack([other], [half])
            response = respond_half(kept, other, swap(other, "mat", 1), masks[1], half, [])
        else:
            pieces = [block, other, beside, swap(other, "mat", 1)]
            response = respond(kept, pieces, masks, [later for later, _ in held[i + 1 :]])
        responses.append([response] + [swap(response, "freq", mask) for mask in range(1, freq_devices)])
    windowed = None
    for i, pieces in enumerate(responses):
        windowed = invert(inverse_spread, onset, pieces, windowed, i * focal, traces.shape)
    return windowed


def solution(mesh):
    placed = (P("freq", None, "mat"), P("freq", None, "mat", None), P(None, "mat"))
    return jax.shard_map(
        on_device, mesh=mesh, in_specs=placed, out_specs=P("freq", None, "mat"), check_vma=False
    )
```
